512 devices in a mesh: lat: 16 (over z, core), lon: 32 (over x, y).
Axes of the slice: x: 4, y: 8, z: 8, core: 2. Of those that a mesh axis runs over, the one named last changes fastest.
Arguments:
- activation: bfloat16 [256, 256, 256], P('lat', 'lon'), may hold values from -6 to 6
- basis_table: bfloat16 [9, 256, 5, 17], replicated, may hold values from -1 to 1
- lat_depth: int32 [256], replicated, may hold values from 1 to 2, as said below
- lon_extent: int32 [256], replicated, may hold values from 1 to 8, as said below
- weight_one: bfloat16 [9, 256, 256], P(None, 'lon'), may hold values from -0.125 to 0.125
- weight_two: bfloat16 [9, 256, 256], P(None, 'lon'), may hold values from -0.125 to 0.125
- cotangent: bfloat16 [256, 256, 256], P('lat', 'lon'), may hold values from -6 to 6
Outputs:
- output: bfloat16 [256, 256, 256], P('lat', 'lon')
- grad_field: bfloat16 [256, 256, 256], P('lat', 'lon')
- grad_one: float32 [9, 256, 256], P(None, 'lon')
- grad_two: float32 [9, 256, 256], P(None, 'lon')
The draws below stay inside these ranges and needn't reach their ends.
Inputs may be any that keep to these rules, and one draw needn't show every extreme that they name: `lat_depth`: the row at index 128 has depth 2. `lon_extent`: the rows nearest the poles reach 8.
All inputs are finite; a program needn't handle non-finite values.
Results may differ from the reference program's by a relative error of at most 0.033.
Values may be sent and summed in bfloat16 or wider, within the bound.
A program may use at most 64 MiB of HBM per device.

```python
import jax
import jax.numpy as jnp
from jax import lax

CHANNELS = 256
BASIS = 9
LAT_REACH = 2
LON_REACH = 8
LAT_DEV = 16
LON_DEV = 8
GRID_LAT = 256
GRID_LON = 256
N_LAT = 16
N_LON = 32


def draw_lat_depth(key, part):
    key = jax.random.fold_in(key, 11)
    row_index = jnp.arange(GRID_LAT, dtype=jnp.int32)
    random_depth = jax.random.randint(key, (GRID_LAT,), 1, LAT_REACH + 1, dtype=jnp.int32)
    return jnp.where(row_index == GRID_LAT // 2, LAT_REACH, random_depth).astype(jnp.int32)


def draw_lon_extent(key, part):
    key = jax.random.fold_in(key, 23)
    row_index = jnp.arange(GRID_LAT, dtype=jnp.int32)
    nearest = jnp.minimum(row_index, GRID_LAT - 1 - row_index)
    random_part = jax.random.randint(key, (GRID_LAT,), 1, LON_REACH // 2 + 1, dtype=jnp.int32)
    widened = random_part + LON_REACH // (1 + nearest)
    return jnp.minimum(LON_REACH, widened).astype(jnp.int32)


def levels(stream_key, dims, pieces, smallest, top_value):
    gain = 1.0
    for axis_at, parts in pieces:
        steps = jax.random.uniform(jax.random.fold_in(jax.random.fold_in(stream_key, 6), axis_at), (parts,), jnp.float32, smallest / len(pieces), top_value / len(pieces))
        gain = gain * jnp.repeat(jnp.exp(steps), dims[axis_at] // parts).reshape((-1,) + (1,) * (len(dims) - 1 - axis_at))
    return gain


def normal_values(own_key, extent, scale, most, cuts=(), held_as=jnp.bfloat16):
    array = jax.random.normal(own_key, extent, jnp.float32) * scale
    if len(cuts) > 0:
        array = levels(own_key, extent, cuts, -0.22, 0.18) * array
    return jnp.clip(array, min=-most, max=most).astype(held_as)


def setup_inputs(seed: int = 0) -> dict:
    keys = jax.random.split(jax.random.key(seed), 8)
    return {
        "activation": normal_values(keys[0], (GRID_LAT, GRID_LON, CHANNELS), 1.0, 6.0, ((0, 16), (1, 32))),
        "basis_table": normal_values(keys[1], (BASIS, GRID_LAT, 2 * LAT_REACH + 1, 2 * LON_REACH + 1), 36 ** -0.5, 1.0),
        "lat_depth": draw_lat_depth(jax.random.fold_in(keys[7], 71), 0),
        "lon_extent": draw_lon_extent(jax.random.fold_in(keys[7], 71), 0),
        "weight_one": normal_values(keys[4], (BASIS, CHANNELS, CHANNELS), (BASIS * CHANNELS) ** -0.5, 0.125, ((1, 32),)),
        "weight_two": normal_values(keys[5], (BASIS, CHANNELS, CHANNELS), (BASIS * CHANNELS) ** -0.5, 0.125, ((1, 32),)),
        "cotangent": normal_values(keys[6], (GRID_LAT, GRID_LON, CHANNELS), 1.0, 6.0, ((0, 16), (1, 32))),
    }


def masked_basis(basis_table, lat_depth, lon_extent):
    lat_span = basis_table.shape[2]
    lon_span = basis_table.shape[3]
    lat_offset = jnp.abs(jnp.arange(lat_span, dtype=jnp.int32) - (lat_span - 1) // 2)
    lon_offset = jnp.abs(jnp.arange(lon_span, dtype=jnp.int32) - (lon_span - 1) // 2)
    inside = (lat_offset[None, :, None] <= lat_depth[:, None, None]) & (lon_offset[None, None, :] <= lon_extent[:, None, None])
    return basis_table * inside.astype(basis_table.dtype)[None]

def pad_field(values, lat_axis):
    widths = [(0, 0)] * values.ndim
    widths[lat_axis] = (LAT_REACH, LAT_REACH)
    padded = jnp.pad(values, widths)
    lon_axis = lat_axis + 1
    left_part = lax.slice_in_dim(padded, GRID_LON - LON_REACH, GRID_LON, axis=lon_axis)
    right_part = lax.slice_in_dim(padded, 0, LON_REACH, axis=lon_axis)
    return jnp.concatenate([left_part, padded, right_part], axis=lon_axis)

def convolve_band(window, coef_band):
    result = jnp.zeros((BASIS, LAT_DEV, GRID_LON, CHANNELS), jnp.float32)
    for lat_step in range(2 * LAT_REACH + 1):
        for lon_step in range(2 * LON_REACH + 1):
            shifted = window[lat_step:lat_step + LAT_DEV, lon_step:lon_step + GRID_LON]
            weight_now = coef_band[:, :, lat_step, lon_step]
            result = result + weight_now[:, :, None, None] * shifted[None]
    return result

def band_state(padded, coefficient, weight, first_row):
    window = lax.dynamic_slice_in_dim(padded, first_row, LAT_DEV + 2 * LAT_REACH, 0).astype(jnp.float32)
    coef_band = lax.dynamic_slice_in_dim(coefficient, first_row, LAT_DEV, 1).astype(jnp.float32)
    mixed_in = convolve_band(window, coef_band).astype(jnp.bfloat16)
    response = jnp.einsum('kljc,kcd->ljd', mixed_in.astype(jnp.float32), weight.astype(jnp.float32))
    return (mixed_in, response)

def forward_layer(values, coefficient, weight):
    padded = pad_field(values, 0)

    def one_band(band_index):
        first_row = band_index * LAT_DEV
        mixed_in, response = band_state(padded, coefficient, weight, first_row)
        own_rows = lax.dynamic_slice_in_dim(values, first_row, LAT_DEV, 0).astype(jnp.float32)
        return (own_rows + jax.nn.gelu(response)).astype(jnp.bfloat16)
    bands = lax.map(one_band, jnp.arange(N_LAT, dtype=jnp.int32))
    return bands.reshape(GRID_LAT, GRID_LON, CHANNELS)

def backward_one(values, coefficient, weight, field_grad):
    padded = pad_field(values, 0)

    def one_step(running, band_index):
        first_row = band_index * LAT_DEV
        mixed_in, response = band_state(padded, coefficient, weight, first_row)
        grad_band = lax.dynamic_slice_in_dim(field_grad, first_row, LAT_DEV, 0).astype(jnp.float32)
        slope_grad = jax.vjp(jax.nn.gelu, response)[1](grad_band)[0].astype(jnp.bfloat16)
        mixed_blocks = mixed_in.astype(jnp.float32).reshape(BASIS, LAT_DEV, N_LON, LON_DEV, CHANNELS)
        slope_blocks = slope_grad.astype(jnp.float32).reshape(LAT_DEV, N_LON, LON_DEV, CHANNELS)
        partials = jnp.einsum('klsjc,lsjd->skcd', mixed_blocks, slope_blocks)
        rounded = lax.optimization_barrier(partials.astype(jnp.bfloat16)).astype(jnp.float32)
        return (running + lax.optimization_barrier(jnp.sum(rounded, axis=0)), slope_grad)
    initial = jnp.zeros((BASIS, CHANNELS, CHANNELS), jnp.float32)
    weight_grad, slopes = lax.scan(one_step, initial, jnp.arange(N_LAT, dtype=jnp.int32))
    return (weight_grad, slopes.reshape(GRID_LAT, GRID_LON, CHANNELS))

def adjoint_band(grad_window, coef_window):
    result = jnp.zeros((LAT_DEV, GRID_LON, CHANNELS), jnp.float32)
    for lat_step in range(2 * LAT_REACH + 1):
        row_first = 2 * LAT_REACH - lat_step
        for lon_step in range(2 * LON_REACH + 1):
            col_first = 2 * LON_REACH - lon_step
            shifted = grad_window[:, row_first:row_first + LAT_DEV, col_first:col_first + GRID_LON]
            weight_now = coef_window[:, row_first:row_first + LAT_DEV, lat_step, lon_step]
            result = result + lax.optimization_barrier(jnp.sum(weight_now[:, :, None, None] * shifted, axis=0))
    return result

def backward_two(slopes, coefficient, weight, field_grad):
    slope_pad = pad_field(slopes, 0)
    coef_pad = jnp.pad(coefficient, ((0, 0), (LAT_REACH, LAT_REACH), (0, 0), (0, 0)))

    def one_band(band_index):
        first_row = band_index * LAT_DEV
        slope_window = lax.dynamic_slice_in_dim(slope_pad, first_row, LAT_DEV + 2 * LAT_REACH, 0).astype(jnp.float32)
        grad_window = jnp.einsum('pqd,kcd->kpqc', slope_window, weight.astype(jnp.float32)).astype(jnp.bfloat16)
        grad_window = lax.optimization_barrier(grad_window).astype(jnp.float32)
        coef_window = lax.dynamic_slice_in_dim(coef_pad, first_row, LAT_DEV + 2 * LAT_REACH, 1).astype(jnp.float32)
        adjoint = adjoint_band(grad_window, coef_window)
        grad_band = lax.dynamic_slice_in_dim(field_grad, first_row, LAT_DEV, 0).astype(jnp.float32)
        return (grad_band + adjoint).astype(jnp.bfloat16)
    bands = lax.map(one_band, jnp.arange(N_LAT, dtype=jnp.int32))
    return bands.reshape(GRID_LAT, GRID_LON, CHANNELS)

def reference(activation, basis_table, lat_depth, lon_extent, weight_one, weight_two, cotangent):
    coefficient = masked_basis(basis_table, lat_depth, lon_extent)
    hidden = forward_layer(activation, coefficient, weight_one)
    output = forward_layer(hidden, coefficient, weight_two)
    grad_two, slope_two = backward_one(hidden, coefficient, weight_two, cotangent)
    grad_hidden = backward_two(slope_two, coefficient, weight_two, cotangent)
    grad_one, slope_one = backward_one(activation, coefficient, weight_one, grad_hidden)
    grad_field = backward_two(slope_one, coefficient, weight_one, grad_hidden)
    return (output, grad_field, grad_one, grad_two)
```

```python
import functools

import jax
import jax.numpy as jnp
from jax import lax
from jax.experimental import pallas as pl
from jax.experimental.pallas import tpu as pltpu
from jax.sharding import PartitionSpec as P

NX, NY, NZ = 4, 8, 8
BASIS = 9
CH = 256
ROWS, COLS = 16, 8
CELLS = ROWS * COLS
GRID = 256
SIDE = (ROWS + 4) * COLS
EXT = 512
OWN = SIDE + 2 * COLS
F32 = jnp.float32
BF16 = jnp.bfloat16
SLOTS = 200


def gelu_and_slope(y):
    c = 0.7978845608028654
    t = jnp.tanh(c * (y + 0.044715 * (y * y * y)))
    cdf = 0.5 * (1.0 + t)
    slope = cdf + 0.5 * y * (1.0 - t * t) * (c * (1.0 + 3.0 * 0.044715 * (y * y)))
    return y * cdf, slope


def kernel(
    act_ref,
    basis_ref,
    depth_ref,
    extent_ref,
    w1_ref,
    w2_ref,
    cot_ref,
    out_ref,
    gfield_ref,
    g1_ref,
    g2_ref,
    bw,
    pad,
    cb,
    t1,
    tmap,
    xs,
    wl,
    wf,
    zb,
    zt,
    zg,
    sg,
    pb,
    ry,
    qy,
    rz,
    fin,
    yb,
    send_sem,
    recv_sem,
    local_sem,
):
    lat = lax.axis_index("lat")
    lon = lax.axis_index("lon")
    z, core = lat // 2, lat % 2
    x, y = lon // NY, lon % NY
    other = 1 - core
    sib = lat + 1 - 2 * core

    def at_x(d):
        return lax.rem(x + d, NX) * NY + y

    def at_y(d):
        return x * NY + lax.rem(y + d + NY, NY)

    def at_z(d):
        return lax.rem(z + d, NZ) * 2 + core

    n_lat, n_lon = 2 * NZ, NX * NY
    lat_up, lat_dn = lax.rem(lat + n_lat - 1, n_lat), lax.rem(lat + 1, n_lat)
    lon_lf, lon_rt = lax.rem(lon + n_lon - 1, n_lon), lax.rem(lon + 1, n_lon)

    barrier = pltpu.get_barrier_semaphore()
    peers = [(sib, lon)]
    peers += [(lat, at_x(d)) for d in range(1, NX)] + [(sib, at_x(d)) for d in range(1, NX)]
    peers += [(lat, at_y(d)) for d in range(1, NY)] + [(at_z(d), lon) for d in range(1, NZ)]
    peers += [(a, b) for a in (lat_up, lat, lat_dn) for b in (lon_lf, lon, lon_rt)
              if not (a is lat and b is lon)]
    for peer in peers:
        pl.semaphore_signal(barrier, inc=1, device_id=peer, device_id_type=pl.DeviceIdType.MESH)

    row0 = lat * ROWS
    loads = [
        pltpu.make_async_copy(basis_ref.at[:, pl.ds(row0, ROWS)], bw.at[:, 2:18], local_sem.at[0]),
        pltpu.make_async_copy(
            basis_ref.at[:, pl.ds(lax.rem(row0 + GRID - 2, GRID), 2)], bw.at[:, 0:2], local_sem.at[1]
        ),
        pltpu.make_async_copy(
            basis_ref.at[:, pl.ds(lax.rem(row0 + ROWS, GRID), 2)], bw.at[:, 18:20], local_sem.at[2]
        ),
    ]
    for load in loads:
        load.start()

    sent = []

    def send(src, dst, device):
        slot = len(sent)
        copy = pltpu.make_async_remote_copy(
            src_ref=src,
            dst_ref=dst,
            send_sem=send_sem.at[slot],
            recv_sem=recv_sem.at[slot],
            device_id=device,
            device_id_type=pl.DeviceIdType.MESH,
        )
        copy.start()
        sent.append(copy)
        return copy

    def arrive(copies):
        for copy in copies:
            copy.wait_recv()

    def flat(ref):
        return ref[...].astype(F32).reshape(CELLS, CH)

    xs[:, 3 * SIDE : EXT, :] = jnp.zeros((4, EXT - 3 * SIDE, CH), BF16)
    xs[0, OWN : OWN + CELLS, :] = flat(act_ref).astype(BF16)
    for w, ref in enumerate((w1_ref, w2_ref)):
        wl[w, core, x, y] = ref[:, :, pl.ds(pl.multiple_of(core * 128, 128), 128)]

    pl.semaphore_wait(barrier, len(peers))

    def halo(n):
        own = xs.at[n, OWN : OWN + CELLS]
        top = xs.at[n, OWN : OWN + 16]
        bottom = xs.at[n, OWN + CELLS - 16 : OWN + CELLS]
        lf, mid, rt = 0, SIDE, 2 * SIDE
        low, high = 16, SIDE - 16

        def to(src, base, off, rows, device):
            return send(src, xs.at[n, base + off : base + off + rows], device)

        return [
            to(own, lf, low, CELLS, (lat, lon_rt)),
            to(own, rt, low, CELLS, (lat, lon_lf)),
            to(bottom, mid, 0, 16, (lat_dn, lon)),
            to(top, mid, high, 16, (lat_up, lon)),
            to(bottom, lf, 0, 16, (lat_dn, lon_rt)),
            to(bottom, rt, 0, 16, (lat_dn, lon_lf)),
            to(top, lf, high, 16, (lat_up, lon_rt)),
            to(top, rt, high, 16, (lat_up, lon_lf)),
        ]

    def share(ref):
        return send(ref, ref, (sib, lon))

    def gather_xy(w, k0, nk):
        ks = slice(k0, k0 + nk)

        def col(dy, xa=0, xb=NX):
            return wl.at[w, core, xa:xb, lax.rem(y + dy + NY, NY), ks]

        mine = wl.at[w, core, x, y, ks]
        got = [send(mine, mine, (lat, at_x(d))) for d in range(1, NX)]
        yield
        arrive(got)
        shared = [share(col(0))]
        half = NX // 2
        for t in range(NY // 2):
            if t < NY // 2 - 1:
                up, dn = col(-t), col(t)
                got_up, got_dn = col(-t - 1), col(t + 1)
            else:
                up, dn = col(-t, 0, half), col(t, half, NX)
                got_up, got_dn = col(-t - 1, 0, half), col(t + 1, half, NX)
            got = [send(up, up, (lat, at_y(1))), send(dn, dn, (lat, at_y(-1)))]
            yield
            arrive(got)
            shared += [share(got_up), share(got_dn)]
        yield
        arrive(shared)

    def gather_yx(w, k0, nk):
        ks = slice(k0, k0 + nk)

        def one(dy, a=0, b=nk):
            return wl.at[w, core, x, lax.rem(y + dy + NY, NY), k0 + a : k0 + b]

        half = nk // 2
        for t in range(NY // 2):
            if t < NY // 2 - 1:
                up, dn = one(-t), one(t)
            else:
                up, dn = one(-t, 0, half), one(t, half, nk)
            got = [send(up, up, (lat, at_y(1))), send(dn, dn, (lat, at_y(-1)))]
            yield
            arrive(got)

        def row(d):
            return wl.at[w, core, lax.rem(x + d, NX), :, ks]

        got = [send(row(0), row(0), (lat, at_x(d))) for d in range(1, NX)]
        shared = [share(row(0))]
        yield
        for d in range(1, NX):
            arrive([got[d - 1]])
            shared.append(share(row(NX - d)))
        yield
        arrive(shared)

    def step(*parts):
        for part in parts:
            next(part, None)

    def finish(*parts):
        live = list(parts)
        while live:
            live = [part for part in live if next(part, "end") != "end"]

    in_halo = halo(0)
    w1_parts = (gather_xy(0, 0, 5), gather_yx(0, 5, 4))
    step(*w1_parts)

    for load in loads:
        load.wait()
    pad[...] = jnp.zeros(pad.shape, F32)
    sub = lax.broadcasted_iota(jnp.int32, (8, 128), 0)
    lane = lax.broadcasted_iota(jnp.int32, (8, 128), 1)
    slot_a = (lane * 2731) >> 16

    def coef_row(r, carry):
        row = row0 + r - 2
        wrapped = lax.rem(row + GRID, GRID)
        inside = (
            (jnp.abs(sub - 2) <= depth_ref[wrapped])
            & (jnp.abs(lane - 8) <= extent_ref[wrapped])
            & (row >= 0)
            & (row < GRID)
        )
        for k in range(BASIS):
            pad[r, k, 0:5, 0:17] = bw[k, r].astype(F32)
        for k in range(BASIS):
            tile = jnp.where(inside, pad[r, k], 0.0)
            tile = pltpu.roll(tile, 0, 1, stride=12, stride_axis=0)
            tile = pltpu.roll(tile, 0, 1, stride=12, stride_axis=0)
            cb[r, k] = jnp.broadcast_to(jnp.sum(tile, axis=0, keepdims=True), (8, 128))
        return carry

    lax.fori_loop(0, ROWS + 4, coef_row, 0)
    step(*w1_parts)

    wide_l = lax.broadcasted_iota(jnp.int32, (256, EXT), 0)
    wide_t = lax.broadcasted_iota(jnp.int32, (256, EXT), 1)
    l_q = wide_l >> 7
    l_in = wide_l & 127
    l_a = (l_in * 2731) >> 16
    l_m = l_in - 24 * l_a

    def build(n):
        def pair(p, carry):
            for q in range(2):
                i = 2 * p + q
                row = row0 + i
                for k in range(BASIS):
                    if n == 0:
                        reach = row + slot_a - 2
                        tile = jnp.where((reach >= 0) & (reach < GRID), cb[i + 2, k], 0.0)
                        tile = pltpu.roll(tile, 0, 1, stride=1, stride_axis=0)
                    else:
                        tile = cb[i + 4, k]
                        for a in range(1, 5):
                            tile = jnp.where(slot_a == a, cb[i + 4 - a, k], tile)
                        tile = pltpu.roll(tile, 0, 1, stride=1, stride_axis=0)
                    t1[p, k, 8 * q : 8 * q + 8, 128 * q : 128 * q + 128] = tile
                    t1[p, k, 8 * q : 8 * q + 8, 128 * (1 - q) : 128 * (1 - q) + 128] = jnp.zeros(
                        (8, 128), F32
                    )
            return carry

        if n == 1:
            src = lax.broadcasted_iota(jnp.int32, (128, 128), 0)
            dst = lax.broadcasted_iota(jnp.int32, (128, 128), 1)
            src_a = (src * 2731) >> 16
            mirror = jnp.where(
                (dst == 48 * src_a + 16 - src) & (src - 24 * src_a < 17) & (src_a < 5), 1.0, 0.0
            ).astype(BF16)
            for r in range(0, ROWS + 4, 4):
                rows = cb[r : r + 4].reshape(4 * BASIS * 8, 128).astype(BF16)
                cb[r : r + 4] = jnp.dot(rows, mirror, preferred_element_type=F32).reshape(
                    4, BASIS, 8, 128
                )
        lax.fori_loop(0, 8, pair, 0)
        m = l_m
        shift = l_q + (l_a if n == 0 else 4 - l_a)
        place = jnp.where(
            (wide_t == (m >> 3) * SIDE + 8 * shift + (m & 7)) & (l_a < 5), 1.0, 0.0
        ).astype(BF16)
        for p in range(8):
            spread = jnp.dot(
                t1[p].reshape(16 * BASIS, 256).astype(BF16), place, preferred_element_type=F32
            )
            spread = pltpu.roll(spread, 16 * p, 1) if p else spread
            tmap[n, :, 16 * p : 16 * p + 16, :] = spread.reshape(BASIS, 16, EXT).astype(BF16)

    build(0)
    step(*w1_parts)

    def conv(n, field):
        for k in range(0, BASIS, 3):
            part = jnp.dot(
                tmap[n, k : k + 3].reshape(3 * CELLS, EXT), xs[field], preferred_element_type=F32
            )
            zb[k : k + 3] = part.astype(BF16).reshape(3, CELLS, CH)

    def spread_z(layer):
        for k in range(BASIS):
            zt[layer, k] = zb[k].astype(F32).T.astype(BF16)

        def block(d):
            return zt.at[layer, :, pl.ds(lax.rem(x + d, NX) * 64, 64)]

        zg[layer, x, core] = zt[layer, :, pl.ds(pl.multiple_of(x * 64, 64), 64)]
        got = [send(block(d), zg.at[layer, x, core], (lat, at_x(d))) for d in range(1, NX)]
        yield
        arrive(got)
        mine = zg.at[layer, :, core]
        shared = [send(mine, mine, (sib, lon))]
        yield
        arrive(shared)

    def settle(w):
        for k in range(BASIS):
            for h in range(2):
                wf[w, k, :, h * 128 : (h + 1) * 128] = (
                    wl[w, h, :, :, k].astype(F32).reshape(CH, 128).astype(BF16)
                )

    def mix(w):
        total = jnp.zeros((CELLS, CH), F32)
        for k in range(BASIS):
            total += jnp.dot(zb[k], wf[w, k], preferred_element_type=F32)
        return total

    def mix_back(w):
        total = jnp.zeros((CELLS, CH), F32)
        for k in range(BASIS):
            total += lax.dot_general(
                zb[k], wf[w, k], (((1,), (1,)), ((), ())), preferred_element_type=F32
            )
        return total

    def own_block(n):
        return xs[n, OWN : OWN + CELLS, :].astype(F32)

    arrive(in_halo)
    conv(0, 0)
    step(*w1_parts)
    build(1)
    finish(*w1_parts)
    settle(0)
    w2_parts = (gather_xy(1, 0, 5), gather_yx(1, 5, 4))
    step(*w2_parts)
    y1 = mix(0)
    yb[...] = y1
    hidden = (own_block(0) + gelu_and_slope(y1)[0]).astype(BF16)
    xs[1, OWN : OWN + CELLS, :] = hidden
    mid_halo = halo(1)
    step(*w2_parts)
    z1 = spread_z(0)
    step(z1)
    step(*w2_parts)
    arrive(mid_halo)
    conv(0, 1)
    finish(*w2_parts)
    settle(1)
    y2 = mix(1)
    grown, slope = gelu_and_slope(y2)
    out_ref[...] = (own_block(1) + grown).reshape(ROWS, COLS, CH).astype(BF16)

    def spread_s(layer, n, values):
        xs[n, OWN : OWN + CELLS, :] = values
        around = halo(n)
        for h in range(2):
            @pl.when(core == h)
            def _():
                sg[layer, x, h] = values[:, h * 128 : (h + 1) * 128]

        got = []
        for d in range(NX):
            for dc in range(2):
                if d == 0 and dc == 0:
                    continue
                h = core if dc == 0 else other
                src = xs.at[n, OWN : OWN + CELLS, pl.ds(pl.multiple_of(h * 128, 128), 128)]
                got.append(
                    send(src, sg.at[layer, x, core], (lat if dc == 0 else sib, at_x(d)))
                )
        return around, got

    around2, all_s2 = spread_s(1, 2, (flat(cot_ref) * slope).astype(BF16))
    z2 = spread_z(1)
    step(z2)
    step(z1)
    arrive(around2)
    conv(1, 2)
    grad_hidden = (flat(cot_ref) + mix_back(1)).astype(BF16).astype(F32)
    s1 = (grad_hidden * gelu_and_slope(yb[...])[1]).astype(BF16)
    around1, all_s1 = spread_s(0, 3, s1)
    step(z2)

    def weight_partial(layer):
        total = jnp.zeros((BASIS * 64, 128), F32)
        for a in range(NX):
            left = jnp.concatenate([zg[layer, a, h].reshape(BASIS * 64, 128) for h in range(2)], axis=1)
            total += jnp.dot(left, sg[layer, a].reshape(256, 128), preferred_element_type=F32)
        blocks = total.reshape(BASIS, NY, 8, 128)
        for b in range(NY):
            pb[layer, b] = blocks[:, b].astype(BF16)
        ry[layer, y] = pb[layer, y]
        return [
            send(pb.at[layer, lax.rem(y + d, NY)], ry.at[layer, y], (lat, at_y(d)))
            for d in range(1, NY)
        ]

    def weight_rows(layer, got):
        arrive(got)
        total = jnp.sum(ry[layer].astype(F32), axis=0)
        qy[layer] = total.astype(BF16)
        rz[layer, z] = qy[layer]
        return [send(qy.at[layer], rz.at[layer, z], (at_z(d), lon)) for d in range(1, NZ)]

    def weight_bands(layer, got):
        arrive(got)
        fin[layer, core] = jnp.sum(rz[layer].astype(F32), axis=0)
        mine = fin.at[layer, core]
        return [send(mine, mine, (sib, lon))]

    arrive(all_s2)
    finish(z1, z2)
    p2 = weight_partial(1)
    arrive(all_s1)
    p1 = weight_partial(0)
    arrive(around1)
    conv(1, 3)
    q2 = weight_rows(1, p2)
    gfield_ref[...] = (grad_hidden + mix_back(0)).reshape(ROWS, COLS, CH).astype(BF16)
    q1 = weight_rows(0, p1)
    r2 = weight_bands(1, q2)
    r1 = weight_bands(0, q1)
    for layer, ref, got in ((1, g2_ref, r2), (0, g1_ref, r1)):
        arrive(got)
        for h in range(2):
            ref[:, :, h * 128 : (h + 1) * 128] = fin[layer, h]
    for copy in sent:
        copy.wait_send()


def local(activation, basis_table, lat_depth, lon_extent, weight_one, weight_two, cotangent):
    vmem = pl.BlockSpec(memory_space=pltpu.VMEM)
    smem = pl.BlockSpec(memory_space=pltpu.SMEM)
    field = jax.ShapeDtypeStruct((ROWS, COLS, CH), BF16)
    grad = jax.ShapeDtypeStruct((BASIS, 8, CH), F32)
    return pl.pallas_call(
        kernel,
        out_shape=(field, field, grad, grad),
        in_specs=[vmem, pl.BlockSpec(memory_space=pl.ANY), smem, smem, vmem, vmem, vmem],
        out_specs=(vmem, vmem, vmem, vmem),
        scratch_shapes=[
            pltpu.VMEM((BASIS, ROWS + 4, 5, 17), BF16),
            pltpu.VMEM((ROWS + 4, BASIS, 8, 128), F32),
            pltpu.VMEM((ROWS + 4, BASIS, 8, 128), F32),
            pltpu.VMEM((8, BASIS, 16, 256), F32),
            pltpu.VMEM((2, BASIS, CELLS, EXT), BF16),
            pltpu.VMEM((4, EXT, CH), BF16),
            pltpu.VMEM((2, 2, NX, NY, BASIS, 8, 128), BF16),
            pltpu.VMEM((2, BASIS, CH, CH), BF16),
            pltpu.VMEM((BASIS, CELLS, CH), BF16),
            pltpu.VMEM((2, BASIS, CH, CELLS), BF16),
            pltpu.VMEM((2, NX, 2, BASIS, 64, CELLS), BF16),
            pltpu.VMEM((2, NX, 2, CELLS, 128), BF16),
            pltpu.VMEM((2, NY, BASIS, 8, 128), BF16),
            pltpu.VMEM((2, NY, BASIS, 8, 128), BF16),
            pltpu.VMEM((2, BASIS, 8, 128), BF16),
            pltpu.VMEM((2, NZ, BASIS, 8, 128), BF16),
            pltpu.VMEM((2, 2, BASIS, 8, 128), F32),
            pltpu.VMEM((CELLS, CH), F32),
            pltpu.SemaphoreType.DMA((SLOTS,)),
            pltpu.SemaphoreType.DMA((SLOTS,)),
            pltpu.SemaphoreType.DMA((3,)),
        ],
        compiler_params=pltpu.CompilerParams(
            collective_id=0, has_side_effects=True, vmem_limit_bytes=48 * 1024 * 1024
        ),
        cost_estimate=pl.CostEstimate(flops=10**9, bytes_accessed=10**7, transcendentals=10**5),
    )(activation, basis_table, lat_depth, lon_extent, weight_one, weight_two, cotangent)


def solution(mesh):
    field = P("lat", "lon", None)
    weight = P(None, "lon", None)
    return jax.shard_map(
        local,
        mesh=mesh,
        in_specs=(field, P(), P(), P(), weight, weight, field),
        out_specs=(field, field, weight, weight),
        check_vma=False,
    )
```

```python
import jax
import jax.numpy as jnp
from jax import lax
from jax.experimental import pallas as pl
from jax.experimental.pallas import tpu as pltpu
from jax.sharding import PartitionSpec as P

NX, NY, NZ = 4, 8, 8
BASIS = 9
CH = 256
ROWS, COLS = 16, 8
CELLS = ROWS * COLS
GRID = 256
SIDE = (ROWS + 4) * COLS
EXT = 512
OWN = SIDE + 2 * COLS
F32 = jnp.float32
BF16 = jnp.bfloat16
SLOTS = 48
SPLIT = 2
PARTS, DEEP = 3, 3


def gelu_and_slope(y):
    c = 0.7978845608028654
    t = jnp.tanh(c * (y + 0.044715 * (y * y * y)))
    cdf = 0.5 * (1.0 + t)
    slope = cdf + 0.5 * y * (1.0 - t * t) * (c * (1.0 + 3.0 * 0.044715 * (y * y)))
    return y * cdf, slope


def kernel(
    act_ref,
    basis_ref,
    depth_ref,
    extent_ref,
    w1_ref,
    w2_ref,
    cot_ref,
    out_ref,
    gfield_ref,
    g1_ref,
    g2_ref,
    basis,
    depth,
    extent,
    cot,
    pad,
    cb,
    t1,
    tmap,
    xs,
    wl,
    wf,
    zb,
    zt,
    zg,
    sg,
    pb,
    ry,
    qy,
    rz,
    fin,
    yb,
    send_sem,
    recv_sem,
    load_sem,
):
    lat = lax.axis_index("lat")
    lon = lax.axis_index("lon")
    z, core = lat // 2, lat % 2
    x, y = lon // NY, lon % NY
    other = 1 - core
    sib = lat + 1 - 2 * core

    def at_x(d):
        return lax.rem(x + d, NX) * NY + y

    def at_y(d):
        return x * NY + lax.rem(y + d, NY)

    def at_z(d):
        return lax.rem(z + d, NZ) * 2 + core

    n_lat, n_lon = 2 * NZ, NX * NY
    lat_up, lat_dn = lax.rem(lat + n_lat - 1, n_lat), lax.rem(lat + 1, n_lat)
    lon_lf, lon_rt = lax.rem(lon + n_lon - 1, n_lon), lax.rem(lon + 1, n_lon)

    barrier = pltpu.get_barrier_semaphore()
    peers = [(sib, lon)]
    peers += [(lat, at_x(d)) for d in range(1, NX)] + [(sib, at_x(d)) for d in range(1, NX)]
    peers += [(lat, at_y(d)) for d in range(1, NY)] + [(at_z(d), lon) for d in range(1, NZ)]
    peers += [
        (a, b)
        for a in (lat_up, lat, lat_dn)
        for b in (lon_lf, lon, lon_rt)
        if not (a is lat and b is lon)
    ]
    for peer in peers:
        pl.semaphore_signal(barrier, inc=1, device_id=peer, device_id_type=pl.DeviceIdType.MESH)

    half = pl.ds(pl.multiple_of(core * 128, 128), 128)
    loads = []

    def load(src, dst):
        copy = pltpu.make_async_copy(src, dst, load_sem.at[len(loads)])
        copy.start()
        loads.append(copy)

    load(w1_ref.at[:, :, half], wl.at[0, core, x, y])
    load(act_ref, xs.at[0, OWN : OWN + CELLS])
    load(basis_ref, basis)
    load(depth_ref, depth)
    load(extent_ref, extent)
    load(w2_ref.at[:, :, half], wl.at[1, core, x, y])
    load(cot_ref, cot)

    sent = []

    def send(copies, whole):
        slot = len(sent)

        def describe(src, dst, device):
            return pltpu.make_async_remote_copy(
                src_ref=src,
                dst_ref=dst,
                send_sem=send_sem.at[slot],
                recv_sem=recv_sem.at[slot],
                device_id=device,
                device_id_type=pl.DeviceIdType.MESH,
            )

        for src, dst, device in copies:
            describe(src, dst, device).start()
        group = describe(whole, whole, (sib, lon))
        sent.append(group)
        return group, describe

    def arrive(group):
        for copy in group[:1]:
            copy.wait_recv()

    xs[:, 3 * SIDE : EXT, :] = jnp.zeros((4, EXT - 3 * SIDE, CH), BF16)
    loads[0].wait()
    loads[1].wait()
    pl.semaphore_wait(barrier, len(peers))

    def halo(n):
        own = xs.at[n, OWN : OWN + CELLS]
        top = xs.at[n, OWN : OWN + 16]
        bottom = xs.at[n, OWN + CELLS - 16 : OWN + CELLS]
        lf, mid, rt = 0, SIDE, 2 * SIDE
        low, high = 16, SIDE - 16

        def to(src, base, off, rows, device):
            return src, xs.at[n, base + off : base + off + rows], device

        return send(
            [
                to(own, lf, low, CELLS, (lat, lon_rt)),
                to(own, rt, low, CELLS, (lat, lon_lf)),
                to(bottom, lf, 0, 16, (lat_dn, lon_rt)),
                to(bottom, rt, 0, 16, (lat_dn, lon_lf)),
                to(top, lf, high, 16, (lat_up, lon_rt)),
                to(top, rt, high, 16, (lat_up, lon_lf)),
                to(bottom, mid, 0, 16, (lat_dn, lon)),
                to(top, mid, high, 16, (lat_up, lon)),
            ],
            xs.at[n, 0 : 2 * CELLS + 6 * 16],
        )

    def gather(w):
        ka, kc = slice(0, SPLIT), slice(SPLIT, BASIS)
        mine_a, mine_c = wl.at[w, core, x, y, ka], wl.at[w, core, x, y, kc]
        first_c = send(
            [(mine_c, mine_c, (lat, at_y(d))) for d in range(1, NY)], wl.at[w, core, x, 0 : NY - 1, kc]
        )
        first_a = send(
            [(mine_a, mine_a, (lat, at_x(d))) for d in range(1, NX)], wl.at[w, core, 0 : NX - 1, y, ka]
        )
        yield
        arrive(first_a)
        column = wl.at[w, core, :, y, ka]
        second_a = send(
            [(column, column, (lat, at_y(d))) for d in range(1, NY)], wl.at[w, core, :, 0 : NY - 1, ka]
        )
        arrive(first_c)

        def row(d):
            return wl.at[w, core, lax.rem(x + d, NX), :, kc]

        second_c = [send([(row(0), row(0), (lat, at_x(d)))], row(0)) for d in range(1, NX)]
        whole = wl.at[w, core]
        shared = send([(row(0), row(0), (sib, lon))], whole)

        def share(ref):
            shared[1](ref, ref, (sib, lon)).start()

        yield
        for d in (1, 3, 2):
            arrive(second_c[d - 1])
            share(row(NX - d))
        arrive(second_a)
        share(wl.at[w, core, :, :, ka])
        yield
        arrive(shared)

    gather1, gather2 = gather(0), gather(1)
    next(gather1)
    in_halo = halo(0)

    for copy in loads[2:5]:
        copy.wait()
    sub = lax.broadcasted_iota(jnp.int32, (8, 128), 0)
    lane = lax.broadcasted_iota(jnp.int32, (8, 128), 1)
    slot_a = (lane * 2731) >> 16
    slot_b = lane - 24 * slot_a
    row0 = lat * ROWS
    picks = 8 * (ROWS + 4)
    pick_row = lax.broadcasted_iota(jnp.int32, (picks, GRID), 0) >> 3
    pick_lane = lax.broadcasted_iota(jnp.int32, (picks, GRID), 1)
    pick = jnp.where(pick_lane == pick_row + row0 - 2, 1.0, 0.0).astype(BF16)
    for k in range(BASIS):
        for a in range(5):
            pad[k, 24 * a : 24 * a + 17, :] = basis[k, a].astype(F32)
        picked = lax.dot_general(
            pick, pad[k].astype(BF16), (((1,), (1,)), ((), ())), preferred_element_type=F32
        )
        cb[:, k] = picked.reshape(ROWS + 4, 8, 128)

    def coef_row(r, carry):
        wrapped = lax.rem(row0 + r + GRID - 2, GRID)
        inside = (
            (jnp.abs(slot_a - 2) <= depth[wrapped])
            & (jnp.abs(slot_b - 8) <= extent[wrapped])
            & (slot_a < 5)
        )
        for k in range(BASIS):
            cb[r, k] = jnp.where(inside, cb[r, k], 0.0)
        return carry

    lax.fori_loop(0, ROWS + 4, coef_row, 0)

    wide_l = lax.broadcasted_iota(jnp.int32, (256, EXT), 0)
    wide_t = lax.broadcasted_iota(jnp.int32, (256, EXT), 1)
    l_q = wide_l >> 7
    l_in = wide_l & 127
    l_a = (l_in * 2731) >> 16
    l_m = l_in - 24 * l_a

    def build(n):
        def pair(p, carry):
            for q in range(2):
                i = 2 * p + q
                row = row0 + i
                for k in range(BASIS):
                    if n == 0:
                        reach = row + slot_a - 2
                        tile = jnp.where((reach >= 0) & (reach < GRID), cb[i + 2, k], 0.0)
                        tile = pltpu.roll(tile, 0, 1, stride=1, stride_axis=0)
                    else:
                        tile = cb[i + 4, k]
                        for a in range(1, 5):
                            tile = jnp.where(slot_a == a, cb[i + 4 - a, k], tile)
                        tile = pltpu.roll(tile, 0, 1, stride=1, stride_axis=0)
                    t1[p, k, 8 * q : 8 * q + 8, 128 * q : 128 * q + 128] = tile
                    t1[p, k, 8 * q : 8 * q + 8, 128 * (1 - q) : 128 * (1 - q) + 128] = jnp.zeros(
                        (8, 128), F32
                    )
            return carry

        if n == 1:
            src = lax.broadcasted_iota(jnp.int32, (128, 128), 0)
            dst = lax.broadcasted_iota(jnp.int32, (128, 128), 1)
            src_a = (src * 2731) >> 16
            mirror = jnp.where(
                (dst == 48 * src_a + 16 - src) & (src - 24 * src_a < 17) & (src_a < 5), 1.0, 0.0
            ).astype(BF16)
            for r in range(0, ROWS + 4, 4):
                rows = cb[r : r + 4].reshape(4 * BASIS * 8, 128).astype(BF16)
                cb[r : r + 4] = jnp.dot(rows, mirror, preferred_element_type=F32).reshape(
                    4, BASIS, 8, 128
                )
        lax.fori_loop(0, 8, pair, 0)
        m = l_m
        shift = l_q + (l_a if n == 0 else 4 - l_a)
        place = jnp.where(
            (wide_t == (m >> 3) * SIDE + 8 * shift + (m & 7)) & (l_a < 5), 1.0, 0.0
        ).astype(BF16)
        for p in range(8):
            spread = jnp.dot(
                t1[p].reshape(16 * BASIS, 256).astype(BF16), place, preferred_element_type=F32
            )
            spread = pltpu.roll(spread, 16 * p, 1) if p else spread
            tmap[n, :, 16 * p : 16 * p + 16, :] = spread.reshape(BASIS, 16, EXT).astype(BF16)

    build(0)

    def conv(n, field):
        for k in range(0, BASIS, 3):
            part = jnp.dot(
                tmap[n, k : k + 3].reshape(3 * CELLS, EXT), xs[field], preferred_element_type=F32
            )
            zb[k : k + 3] = part.astype(BF16).reshape(3, CELLS, CH)

    def spread_z(layer):
        for k in range(BASIS):
            zt[layer, k] = zb[k].astype(F32).T.astype(BF16)

        def block(d):
            return zt.at[layer, :, pl.ds(lax.rem(x + d, NX) * 64, 64)]

        zg[layer, x, core] = zt[layer, :, pl.ds(pl.multiple_of(x * 64, 64), 64)]
        got = send(
            [(block(d), zg.at[layer, x, core], (lat, at_x(d))) for d in range(1, NX)],
            zg.at[layer, 0 : NX - 1, core],
        )
        yield
        arrive(got)
        mine = zg.at[layer, :, core]
        shared = send([(mine, mine, (sib, lon))], mine)
        yield
        arrive(shared)

    def settle(w):
        for k in range(BASIS):
            for h in range(2):
                wf[w, k, :, h * 128 : (h + 1) * 128] = (
                    wl[w, h, :, :, k].astype(F32).reshape(CH, 128).astype(BF16)
                )

    def mix(w):
        total = jnp.zeros((CELLS, CH), F32)
        for k in range(BASIS):
            total += jnp.dot(zb[k], wf[w, k], preferred_element_type=F32)
        return total

    def mix_back(w):
        total = jnp.zeros((CELLS, CH), F32)
        for k in range(BASIS):
            total += lax.dot_general(
                zb[k], wf[w, k], (((1,), (1,)), ((), ())), preferred_element_type=F32
            )
        return total

    def own_block(n):
        return xs[n, OWN : OWN + CELLS, :].astype(F32)

    def spread_s(layer, n, values):
        xs[n, OWN : OWN + CELLS, :] = values
        around = halo(n)
        for h in range(2):

            @pl.when(core == h)
            def _():
                sg[layer, x, h] = values[:, h * 128 : (h + 1) * 128]

        copies = []
        for d in (1, 3, 2, 0):
            for dc in range(2):
                if d == 0 and dc == 0:
                    continue
                h = core if dc == 0 else other
                src = xs.at[n, OWN : OWN + CELLS, pl.ds(pl.multiple_of(h * 128, 128), 128)]
                copies.append((src, sg.at[layer, x, core], (lat if dc == 0 else sib, at_x(d))))
        return around, send(copies, xs.at[n, 0 : 7 * CELLS // 2])

    def weight_partial(layer):
        groups = []
        for c in range(PARTS):
            total = jnp.zeros((DEEP * 64, 128), F32)
            ks = slice(DEEP * c, DEEP * c + DEEP)
            for a in range(NX):
                left = jnp.concatenate(
                    [zg[layer, a, h, ks].reshape(DEEP * 64, 128) for h in range(2)], axis=1
                )
                total += jnp.dot(left, sg[layer, a].reshape(256, 128), preferred_element_type=F32)
            blocks = total.reshape(DEEP, NY, 8, 128)
            for b in range(NY):
                pb[layer, c, b] = blocks[:, b].astype(BF16)
            ry[layer, c, y] = pb[layer, c, y]
            groups.append(
                send(
                    [
                        (pb.at[layer, c, lax.rem(y + d, NY)], ry.at[layer, c, y], (lat, at_y(d)))
                        for d in (4, 3, 5, 2, 6, 1, 7)
                    ],
                    ry.at[layer, c, 0 : NY - 1],
                )
            )
        return groups

    def weight_rows(layer, got):
        groups = []
        for c in range(PARTS):
            arrive(got[c])
            qy[layer, c] = jnp.sum(ry[layer, c].astype(F32), axis=0).astype(BF16)
            rz[layer, c, z] = qy[layer, c]
            groups.append(
                send(
                    [
                        (qy.at[layer, c], rz.at[layer, c, z], (at_z(d), lon))
                        for d in (4, 3, 5, 2, 6, 1, 7)
                    ],
                    rz.at[layer, c, 0 : NZ - 1],
                )
            )
        return groups

    def weight_bands(layer, got):
        groups = []
        for c in range(PARTS):
            arrive(got[c])
            ks = slice(DEEP * c, DEEP * c + DEEP)
            fin[layer, core, ks] = jnp.sum(rz[layer, c].astype(F32), axis=0)
            mine = fin.at[layer, core, ks]
            groups.append(send([(mine, mine, (sib, lon))], mine))
        return groups

    next(gather1)
    loads[5].wait()
    next(gather2)
    build(1)
    arrive(in_halo)
    conv(0, 0)
    next(gather2)
    next(gather1)
    next(gather1, None)
    settle(0)
    y1 = mix(0)
    yb[...] = y1
    hidden = (own_block(0) + gelu_and_slope(y1)[0]).astype(BF16)
    xs[1, OWN : OWN + CELLS, :] = hidden
    mid_halo = halo(1)
    z1 = spread_z(0)
    next(z1)
    next(gather2)
    next(gather2, None)
    settle(1)
    arrive(mid_halo)
    conv(0, 1)
    y2 = mix(1)
    grown, slope = gelu_and_slope(y2)
    loads[6].wait()
    around2, all_s2 = spread_s(1, 2, (cot[...].astype(F32) * slope).astype(BF16))
    out_ref[...] = (own_block(1) + grown).astype(BF16)
    z2 = spread_z(1)
    next(z2)
    next(z1)
    arrive(around2)
    conv(1, 2)
    grad_hidden = (cot[...].astype(F32) + mix_back(1)).astype(BF16).astype(F32)
    s1 = (grad_hidden * gelu_and_slope(yb[...])[1]).astype(BF16)
    around1, all_s1 = spread_s(0, 3, s1)
    next(z2)
    arrive(all_s2)
    next(z1, None)
    next(z2, None)
    p2 = weight_partial(1)
    arrive(all_s1)
    p1 = weight_partial(0)
    arrive(around1)
    conv(1, 3)
    q2 = weight_rows(1, p2)
    gfield_ref[...] = (grad_hidden + mix_back(0)).astype(BF16)
    q1 = weight_rows(0, p1)
    r2 = weight_bands(1, q2)
    r1 = weight_bands(0, q1)
    for layer, ref, got in ((1, g2_ref, r2), (0, g1_ref, r1)):
        for group in got:
            arrive(group)
        for h in range(2):
            ref[:, :, h * 128 : (h + 1) * 128] = fin[layer, h]
    for copy in sent:
        copy.wait_send()


def deliver(*refs):
    count = len(refs) // 2
    for src, dst in zip(refs[:count], refs[count:]):
        dst[...] = src[...]


def local(activation, basis_table, lat_depth, lon_extent, weight_one, weight_two, cotangent):
    vmem = pl.BlockSpec(memory_space=pltpu.VMEM)
    hbm = pl.BlockSpec(memory_space=pltpu.HBM)
    field = jax.ShapeDtypeStruct((CELLS, CH), BF16)
    grad = jax.ShapeDtypeStruct((BASIS, 8, CH), F32)
    shapes = (field, field, grad, grad)
    results = pl.pallas_call(
        kernel,
        out_shape=shapes,
        in_specs=[hbm] * 7,
        out_specs=(vmem,) * 4,
        scratch_shapes=[
            pltpu.VMEM((BASIS, 5, 17, GRID), BF16),
            pltpu.SMEM((GRID,), jnp.int32),
            pltpu.SMEM((GRID,), jnp.int32),
            pltpu.VMEM((CELLS, CH), BF16),
            pltpu.VMEM((BASIS, 128, GRID), F32),
            pltpu.VMEM((ROWS + 4, BASIS, 8, 128), F32),
            pltpu.VMEM((8, BASIS, 16, 256), F32),
            pltpu.VMEM((2, BASIS, CELLS, EXT), BF16),
            pltpu.VMEM((4, EXT, CH), BF16),
            pltpu.VMEM((2, 2, NX, NY, BASIS, 8, 128), BF16),
            pltpu.VMEM((2, BASIS, CH, CH), BF16),
            pltpu.VMEM((BASIS, CELLS, CH), BF16),
            pltpu.VMEM((2, BASIS, CH, CELLS), BF16),
            pltpu.VMEM((2, NX, 2, BASIS, 64, CELLS), BF16),
            pltpu.VMEM((2, NX, 2, CELLS, 128), BF16),
            pltpu.VMEM((2, PARTS, NY, DEEP, 8, 128), BF16),
            pltpu.VMEM((2, PARTS, NY, DEEP, 8, 128), BF16),
            pltpu.VMEM((2, PARTS, DEEP, 8, 128), BF16),
            pltpu.VMEM((2, PARTS, NZ, DEEP, 8, 128), BF16),
            pltpu.VMEM((2, 2, BASIS, 8, 128), F32),
            pltpu.VMEM((CELLS, CH), F32),
            pltpu.SemaphoreType.DMA((SLOTS,)),
            pltpu.SemaphoreType.DMA((SLOTS,)),
            pltpu.SemaphoreType.DMA((7,)),
        ],
        compiler_params=pltpu.CompilerParams(
            collective_id=0, has_side_effects=True, vmem_limit_bytes=63 * 1024 * 1024
        ),
        cost_estimate=pl.CostEstimate(flops=10**9, bytes_accessed=10**7, transcendentals=10**5),
    )(
        activation.reshape(CELLS, CH),
        jnp.transpose(basis_table, (0, 2, 3, 1)),
        lat_depth,
        lon_extent,
        weight_one,
        weight_two,
        cotangent.reshape(CELLS, CH),
    )
    out, grad_field, grad_one, grad_two = pl.pallas_call(
        deliver,
        out_shape=shapes,
        in_specs=[vmem] * 4,
        out_specs=(vmem,) * 4,
    )(*results)
    block = (ROWS, COLS, CH)
    return out.reshape(block), grad_field.reshape(block), grad_one, grad_two


def solution(mesh):
    field = P("lat", "lon", None)
    weight = P(None, "lon", None)
    return jax.shard_map(
        local,
        mesh=mesh,
        in_specs=(field, P(), P(), P(), weight, weight, field),
        out_specs=(field, field, weight, weight),
        check_vma=False,
    )
```

```python
import jax
import jax.numpy as jnp
from jax import lax
from jax.experimental import pallas as pl
from jax.experimental.pallas import tpu as pltpu
from jax.sharding import PartitionSpec as P

NX, NY, NZ = 4, 8, 8
BASIS = 9
CH = 256
ROWS, COLS = 16, 8
CELLS = ROWS * COLS
GRID = 256
SIDE = (ROWS + 4) * COLS
EXT = 512
OWN = SIDE + 2 * COLS
F32 = jnp.float32
BF16 = jnp.bfloat16
SLOTS = 60
SPLIT = 2
PARTS, DEEP = 3, 3


def gelu_and_slope(y):
    c = 0.7978845608028654
    t = jnp.tanh(c * (y + 0.044715 * (y * y * y)))
    cdf = 0.5 * (1.0 + t)
    slope = cdf + 0.5 * y * (1.0 - t * t) * (c * (1.0 + 3.0 * 0.044715 * (y * y)))
    return y * cdf, slope


def kernel(
    act_ref,
    basis_ref,
    depth_ref,
    extent_ref,
    w1_ref,
    w2_ref,
    cot_ref,
    out_ref,
    gfield_ref,
    g1_ref,
    g2_ref,
    basis,
    depth,
    extent,
    cot,
    pad,
    cb,
    t1,
    tmap,
    xs,
    wl,
    wf,
    zb,
    xt,
    xg,
    zg,
    sg,
    pb,
    ry,
    qy,
    rz,
    fin,
    yb,
    send_sem,
    recv_sem,
    load_sem,
):
    lat = lax.axis_index("lat")
    lon = lax.axis_index("lon")
    z, core = lat // 2, lat % 2
    x, y = lon // NY, lon % NY
    other = 1 - core
    sib = lat + 1 - 2 * core

    def at_x(d):
        return lax.rem(x + d, NX) * NY + y

    def at_y(d):
        return x * NY + lax.rem(y + d, NY)

    def at_z(d):
        return lax.rem(z + d, NZ) * 2 + core

    n_lat, n_lon = 2 * NZ, NX * NY
    lat_up, lat_dn = lax.rem(lat + n_lat - 1, n_lat), lax.rem(lat + 1, n_lat)
    lon_lf, lon_rt = lax.rem(lon + n_lon - 1, n_lon), lax.rem(lon + 1, n_lon)

    barrier = pltpu.get_barrier_semaphore()
    peers = [(sib, lon)]
    peers += [(lat, at_x(d)) for d in range(1, NX)] + [(sib, at_x(d)) for d in range(1, NX)]
    peers += [(lat, at_y(d)) for d in range(1, NY)] + [(at_z(d), lon) for d in range(1, NZ)]
    peers += [
        (a, b)
        for a in (lat_up, lat, lat_dn)
        for b in (lon_lf, lon, lon_rt)
        if not (a is lat and b is lon)
    ]
    for peer in peers:
        pl.semaphore_signal(barrier, inc=1, device_id=peer, device_id_type=pl.DeviceIdType.MESH)

    half = pl.ds(pl.multiple_of(core * 128, 128), 128)
    loads = []

    def load(src, dst):
        copy = pltpu.make_async_copy(src, dst, load_sem.at[len(loads)])
        copy.start()
        loads.append(copy)

    load(w1_ref.at[:, :, half], wl.at[0, core, x, y])
    load(act_ref, xs.at[0, OWN : OWN + CELLS])
    load(basis_ref, basis)
    load(depth_ref, depth)
    load(extent_ref, extent)
    load(w2_ref.at[:, :, half], wl.at[1, core, x, y])
    load(cot_ref, cot)

    sent = []

    def send(copies, whole):
        slot = len(sent)

        def describe(src, dst, device):
            return pltpu.make_async_remote_copy(
                src_ref=src,
                dst_ref=dst,
                send_sem=send_sem.at[slot],
                recv_sem=recv_sem.at[slot],
                device_id=device,
                device_id_type=pl.DeviceIdType.MESH,
            )

        for src, dst, device in copies:
            describe(src, dst, device).start()
        group = describe(whole, whole, (sib, lon))
        sent.append(group)
        return group

    def arrive(*groups):
        for copy in groups:
            copy.wait_recv()

    xs[:, 3 * SIDE : EXT, :] = jnp.zeros((4, EXT - 3 * SIDE, CH), BF16)
    loads[0].wait()
    loads[1].wait()
    pl.semaphore_wait(barrier, len(peers))

    def halo(n):
        own = xs.at[n, OWN : OWN + CELLS]
        top = xs.at[n, OWN : OWN + 16]
        bottom = xs.at[n, OWN + CELLS - 16 : OWN + CELLS]
        lf, mid, rt = 0, SIDE, 2 * SIDE
        low, high = 16, SIDE - 16

        def to(src, base, off, rows, device):
            return src, xs.at[n, base + off : base + off + rows], device

        return send(
            [
                to(own, lf, low, CELLS, (lat, lon_rt)),
                to(own, rt, low, CELLS, (lat, lon_lf)),
                to(bottom, lf, 0, 16, (lat_dn, lon_rt)),
                to(bottom, rt, 0, 16, (lat_dn, lon_lf)),
                to(top, lf, high, 16, (lat_up, lon_rt)),
                to(top, rt, high, 16, (lat_up, lon_lf)),
                to(bottom, mid, 0, 16, (lat_dn, lon)),
                to(top, mid, high, 16, (lat_up, lon)),
            ],
            xs.at[n, 0 : 2 * CELLS + 6 * 16],
        )

    def gather(w):
        ka, kc = slice(0, SPLIT), slice(SPLIT, BASIS)
        mine_a, mine_c = wl.at[w, core, x, y, ka], wl.at[w, core, x, y, kc]
        first_c = send(
            [(mine_c, mine_c, (lat, at_y(d))) for d in range(1, NY)], wl.at[w, core, x, 0 : NY - 1, kc]
        )
        first_a = send(
            [(mine_a, mine_a, (lat, at_x(d))) for d in range(1, NX)], wl.at[w, core, 0 : NX - 1, y, ka]
        )
        yield
        arrive(first_a)
        column = wl.at[w, core, :, y, ka]
        second_a = send(
            [(column, column, (lat, at_y(d))) for d in range(1, NY)], wl.at[w, core, :, 0 : NY - 1, ka]
        )
        arrive(first_c)

        def row(d):
            return wl.at[w, core, lax.rem(x + d, NX), :, kc]

        second_c = [send([(row(0), row(0), (lat, at_x(d)))], row(0)) for d in range(1, NX)]
        shared = []

        def share(ref):
            shared.append(send([(ref, ref, (sib, lon))], ref))

        share(row(0))
        yield
        for d in (1, 3, 2):
            arrive(second_c[d - 1])
            share(row(NX - d))
        arrive(second_a)
        share(wl.at[w, core, :, :, ka])
        yield
        arrive(*shared)

    gather1, gather2 = gather(0), gather(1)
    next(gather1)
    in_halo = halo(0)
    loads[5].wait()
    next(gather2)

    for copy in loads[2:5]:
        copy.wait()
    sub = lax.broadcasted_iota(jnp.int32, (8, 128), 0)
    lane = lax.broadcasted_iota(jnp.int32, (8, 128), 1)
    slot_a = (lane * 2731) >> 16
    slot_b = lane - 24 * slot_a
    row0 = lat * ROWS
    picks = 8 * (ROWS + 4)
    pick_row = lax.broadcasted_iota(jnp.int32, (picks, GRID), 0) >> 3
    pick_lane = lax.broadcasted_iota(jnp.int32, (picks, GRID), 1)
    pick = jnp.where(pick_lane == pick_row + row0 - 2, 1.0, 0.0).astype(BF16)
    for k in range(BASIS):
        for a in range(5):
            pad[k, 24 * a : 24 * a + 17, :] = basis[k, a].astype(F32)
        picked = lax.dot_general(
            pick, pad[k].astype(BF16), (((1,), (1,)), ((), ())), preferred_element_type=F32
        )
        cb[:, k] = picked.reshape(ROWS + 4, 8, 128)

    def coef_row(r, carry):
        wrapped = lax.rem(row0 + r + GRID - 2, GRID)
        inside = (
            (jnp.abs(slot_a - 2) <= depth[wrapped])
            & (jnp.abs(slot_b - 8) <= extent[wrapped])
            & (slot_a < 5)
        )
        for k in range(BASIS):
            cb[r, k] = jnp.where(inside, cb[r, k], 0.0)
        return carry

    lax.fori_loop(0, ROWS + 4, coef_row, 0)

    wide_l = lax.broadcasted_iota(jnp.int32, (256, EXT), 0)
    wide_t = lax.broadcasted_iota(jnp.int32, (256, EXT), 1)
    l_q = wide_l >> 7
    l_in = wide_l & 127
    l_a = (l_in * 2731) >> 16
    l_m = l_in - 24 * l_a

    def build(n):
        def pair(p, carry):
            for q in range(2):
                i = 2 * p + q
                row = row0 + i
                for k in range(BASIS):
                    if n == 0:
                        reach = row + slot_a - 2
                        tile = jnp.where((reach >= 0) & (reach < GRID), cb[i + 2, k], 0.0)
                        tile = pltpu.roll(tile, 0, 1, stride=1, stride_axis=0)
                    else:
                        tile = cb[i + 4, k]
                        for a in range(1, 5):
                            tile = jnp.where(slot_a == a, cb[i + 4 - a, k], tile)
                        tile = pltpu.roll(tile, 0, 1, stride=1, stride_axis=0)
                    t1[p, k, 8 * q : 8 * q + 8, 128 * q : 128 * q + 128] = tile
                    t1[p, k, 8 * q : 8 * q + 8, 128 * (1 - q) : 128 * (1 - q) + 128] = jnp.zeros(
                        (8, 128), F32
                    )
            return carry

        if n == 1:
            src = lax.broadcasted_iota(jnp.int32, (128, 128), 0)
            dst = lax.broadcasted_iota(jnp.int32, (128, 128), 1)
            src_a = (src * 2731) >> 16
            mirror = jnp.where(
                (dst == 48 * src_a + 16 - src) & (src - 24 * src_a < 17) & (src_a < 5), 1.0, 0.0
            ).astype(BF16)
            for r in range(0, ROWS + 4, 4):
                rows = cb[r : r + 4].reshape(4 * BASIS * 8, 128).astype(BF16)
                cb[r : r + 4] = jnp.dot(rows, mirror, preferred_element_type=F32).reshape(
                    4, BASIS, 8, 128
                )
        lax.fori_loop(0, 8, pair, 0)
        m = l_m
        shift = l_q + (l_a if n == 0 else 4 - l_a)
        place = jnp.where(
            (wide_t == (m >> 3) * SIDE + 8 * shift + (m & 7)) & (l_a < 5), 1.0, 0.0
        ).astype(BF16)
        for p in range(8):
            spread = jnp.dot(
                t1[p].reshape(16 * BASIS, 256).astype(BF16), place, preferred_element_type=F32
            )
            spread = pltpu.roll(spread, 16 * p, 1) if p else spread
            tmap[n, :, 16 * p : 16 * p + 16, :] = spread.reshape(BASIS, 16, EXT).astype(BF16)

    build(0)

    def conv(n, field):
        for k in range(0, BASIS, 3):
            part = jnp.dot(
                tmap[n, k : k + 3].reshape(3 * CELLS, EXT), xs[field], preferred_element_type=F32
            )
            zb[k : k + 3] = part.astype(BF16).reshape(3, CELLS, CH)

    def spread_x(layer):
        xt[layer] = xs[layer].astype(F32).T.astype(BF16)
        xg[layer, x] = xt[layer, pl.ds(pl.multiple_of(x * 64, 64), 64)]

        def block(d):
            return xt.at[layer, pl.ds(pl.multiple_of(lax.rem(x + d, NX) * 64, 64), 64)]

        got = send(
            [(block(d), xg.at[layer, x], (lat, at_x(d))) for d in (2, 1, 3)],
            xg.at[layer, 0 : NX - 1],
        )
        yield
        arrive(got)
        for k in range(0, BASIS, 3):
            part = lax.dot_general(
                xg[layer].reshape(NX * 64, EXT),
                tmap[0, k : k + 3].reshape(3 * CELLS, EXT),
                (((1,), (1,)), ((), ())),
                preferred_element_type=F32,
            ).astype(BF16)
            for a in range(NX):
                for b in range(3):
                    zg[layer, a, core, k + b] = part[
                        64 * a : 64 * a + 64, CELLS * b : CELLS * b + CELLS
                    ]
        mine = zg.at[layer, :, core]
        shared = send([(mine, mine, (sib, lon))], mine)
        yield
        arrive(shared)

    def settle(w):
        for k in range(BASIS):
            for h in range(2):
                wf[w, k, :, h * 128 : (h + 1) * 128] = (
                    wl[w, h, :, :, k].astype(F32).reshape(CH, 128).astype(BF16)
                )

    def mix(w):
        total = jnp.zeros((CELLS, CH), F32)
        for k in range(BASIS):
            total += jnp.dot(zb[k], wf[w, k], preferred_element_type=F32)
        return total

    def mix_back(w):
        total = jnp.zeros((CELLS, CH), F32)
        for k in range(BASIS):
            total += lax.dot_general(
                zb[k], wf[w, k], (((1,), (1,)), ((), ())), preferred_element_type=F32
            )
        return total

    def own_block(n):
        return xs[n, OWN : OWN + CELLS, :].astype(F32)

    def spread_s(layer, n, values):
        xs[n, OWN : OWN + CELLS, :] = values
        if layer:
            around = halo(n)
        for h in range(2):

            @pl.when(core == h)
            def _():
                sg[layer, x, h] = values[:, h * 128 : (h + 1) * 128]

        copies = []
        for d in (1, 3, 2, 0):
            for dc in range(2):
                if d == 0 and dc == 0:
                    continue
                h = core if dc == 0 else other
                src = xs.at[n, OWN : OWN + CELLS, pl.ds(pl.multiple_of(h * 128, 128), 128)]
                copies.append((src, sg.at[layer, x, core], (lat if dc == 0 else sib, at_x(d))))
        spread = send(copies, xs.at[n, 0 : 7 * CELLS // 2])
        if not layer:
            around = halo(n)
        return around, spread

    def weight_partial(layer):
        groups = []
        for c in range(PARTS):
            total = jnp.zeros((DEEP * 64, 128), F32)
            ks = slice(DEEP * c, DEEP * c + DEEP)
            for a in range(NX):
                left = jnp.concatenate(
                    [zg[layer, a, h, ks].reshape(DEEP * 64, 128) for h in range(2)], axis=1
                )
                total += jnp.dot(left, sg[layer, a].reshape(256, 128), preferred_element_type=F32)
            blocks = total.reshape(DEEP, NY, 8, 128)
            for b in range(NY):
                pb[layer, c, b] = blocks[:, b].astype(BF16)
            ry[layer, c, y] = pb[layer, c, y]
            groups.append(
                send(
                    [
                        (pb.at[layer, c, lax.rem(y + d, NY)], ry.at[layer, c, y], (lat, at_y(d)))
                        for d in (4, 3, 5, 2, 6, 1, 7)
                    ],
                    ry.at[layer, c, 0 : NY - 1],
                )
            )
        return groups

    def weight_rows(layer, got):
        groups = []
        for c in range(PARTS):
            arrive(got[c])
            qy[layer, c] = jnp.sum(ry[layer, c].astype(F32), axis=0).astype(BF16)
            rz[layer, c, z] = qy[layer, c]
            groups.append(
                send(
                    [
                        (qy.at[layer, c], rz.at[layer, c, z], (at_z(d), lon))
                        for d in (4, 3, 5, 2, 6, 1, 7)
                    ],
                    rz.at[layer, c, 0 : NZ - 1],
                )
            )
        return groups

    def weight_bands(layer, got):
        groups = []
        for c in range(PARTS):
            arrive(got[c])
            ks = slice(DEEP * c, DEEP * c + DEEP)
            fin[layer, core, ks] = jnp.sum(rz[layer, c].astype(F32), axis=0)
            mine = fin.at[layer, core, ks]
            groups.append(send([(mine, mine, (sib, lon))], mine))
        return groups

    next(gather1)
    build(1)
    next(gather2)
    arrive(in_halo)
    conv(0, 0)
    next(gather1)
    next(gather1, None)
    settle(0)
    y1 = mix(0)
    yb[...] = y1
    hidden = (own_block(0) + gelu_and_slope(y1)[0]).astype(BF16)
    xs[1, OWN : OWN + CELLS, :] = hidden
    mid_halo = halo(1)
    z1 = spread_x(0)
    next(z1)
    next(gather2)
    next(gather2, None)
    settle(1)
    next(z1)
    arrive(mid_halo)
    conv(0, 1)
    z2 = spread_x(1)
    next(z2)
    y2 = mix(1)
    grown, slope = gelu_and_slope(y2)
    loads[6].wait()
    around2, all_s2 = spread_s(1, 2, (cot[...].astype(F32) * slope).astype(BF16))
    out_ref[...] = (own_block(1) + grown).astype(BF16)
    next(z2)
    arrive(around2)
    conv(1, 2)
    grad_hidden = (cot[...].astype(F32) + mix_back(1)).astype(BF16).astype(F32)
    s1 = (grad_hidden * gelu_and_slope(yb[...])[1]).astype(BF16)
    around1, all_s1 = spread_s(0, 3, s1)
    arrive(all_s2)
    next(z1, None)
    next(z2, None)
    p2 = weight_partial(1)
    arrive(all_s1)
    p1 = weight_partial(0)
    arrive(around1)
    conv(1, 3)
    q2 = weight_rows(1, p2)
    gfield_ref[...] = (grad_hidden + mix_back(0)).astype(BF16)
    q1 = weight_rows(0, p1)
    r2 = weight_bands(1, q2)
    r1 = weight_bands(0, q1)
    for layer, ref, got in ((1, g2_ref, r2), (0, g1_ref, r1)):
        for group in got:
            arrive(group)
        for h in range(2):
            ref[:, :, h * 128 : (h + 1) * 128] = fin[layer, h]
    for copy in sent:
        copy.wait_send()


def deliver(*refs):
    count = len(refs) // 2
    for src, dst in zip(refs[:count], refs[count:]):
        dst[...] = src[...]


def local(activation, basis_table, lat_depth, lon_extent, weight_one, weight_two, cotangent):
    vmem = pl.BlockSpec(memory_space=pltpu.VMEM)
    hbm = pl.BlockSpec(memory_space=pltpu.HBM)
    field = jax.ShapeDtypeStruct((CELLS, CH), BF16)
    grad = jax.ShapeDtypeStruct((BASIS, 8, CH), F32)
    shapes = (field, field, grad, grad)
    results = pl.pallas_call(
        kernel,
        out_shape=shapes,
        in_specs=[hbm] * 7,
        out_specs=(vmem,) * 4,
        scratch_shapes=[
            pltpu.VMEM((BASIS, 5, 17, GRID), BF16),
            pltpu.SMEM((GRID,), jnp.int32),
            pltpu.SMEM((GRID,), jnp.int32),
            pltpu.VMEM((CELLS, CH), BF16),
            pltpu.VMEM((BASIS, 128, GRID), F32),
            pltpu.VMEM((ROWS + 4, BASIS, 8, 128), F32),
            pltpu.VMEM((8, BASIS, 16, 256), F32),
            pltpu.VMEM((2, BASIS, CELLS, EXT), BF16),
            pltpu.VMEM((4, EXT, CH), BF16),
            pltpu.VMEM((2, 2, NX, NY, BASIS, 8, 128), BF16),
            pltpu.VMEM((2, BASIS, CH, CH), BF16),
            pltpu.VMEM((BASIS, CELLS, CH), BF16),
            pltpu.VMEM((2, CH, EXT), BF16),
            pltpu.VMEM((2, NX, 64, EXT), BF16),
            pltpu.VMEM((2, NX, 2, BASIS, 64, CELLS), BF16),
            pltpu.VMEM((2, NX, 2, CELLS, 128), BF16),
            pltpu.VMEM((2, PARTS, NY, DEEP, 8, 128), BF16),
            pltpu.VMEM((2, PARTS, NY, DEEP, 8, 128), BF16),
            pltpu.VMEM((2, PARTS, DEEP, 8, 128), BF16),
            pltpu.VMEM((2, PARTS, NZ, DEEP, 8, 128), BF16),
            pltpu.VMEM((2, 2, BASIS, 8, 128), F32),
            pltpu.VMEM((CELLS, CH), F32),
            pltpu.SemaphoreType.DMA((SLOTS,)),
            pltpu.SemaphoreType.DMA((SLOTS,)),
            pltpu.SemaphoreType.DMA((7,)),
        ],
        compiler_params=pltpu.CompilerParams(
            collective_id=0, has_side_effects=True, vmem_limit_bytes=63 * 1024 * 1024
        ),
        cost_estimate=pl.CostEstimate(flops=10**9, bytes_accessed=10**7, transcendentals=10**5),
    )(
        activation.reshape(CELLS, CH),
        jnp.transpose(basis_table, (0, 2, 3, 1)),
        lat_depth,
        lon_extent,
        weight_one,
        weight_two,
        cotangent.reshape(CELLS, CH),
    )
    out, grad_field, grad_one, grad_two = pl.pallas_call(
        deliver,
        out_shape=shapes,
        in_specs=[vmem] * 4,
        out_specs=(vmem,) * 4,
    )(*results)
    block = (ROWS, COLS, CH)
    return out.reshape(block), grad_field.reshape(block), grad_one, grad_two


def solution(mesh):
    field = P("lat", "lon", None)
    weight = P(None, "lon", None)
    return jax.shard_map(
        local,
        mesh=mesh,
        in_specs=(field, P(), P(), P(), weight, weight, field),
        out_specs=(field, field, weight, weight),
        check_vma=False,
    )
```

```python
import jax
import jax.numpy as jnp
from jax import lax
from jax.experimental import pallas as pl
from jax.experimental.pallas import tpu as pltpu
from jax.sharding import PartitionSpec as P

NX, NY, NZ = 4, 8, 8
BASIS = 9
CH = 256
ROWS, COLS = 16, 8
CELLS = ROWS * COLS
GRID = 256
SIDE = (ROWS + 8) * COLS
EXT = 640
OWN = SIDE + 4 * COLS
WIDE = (ROWS + 4) * COLS
FIRST = 1024
F32 = jnp.float32
BF16 = jnp.bfloat16
SLOTS = 60
SPLIT = 1
PARTS, DEEP = 3, 3


def gelu_and_slope(y):
    c = 0.7978845608028654
    t = jnp.tanh(c * (y + 0.044715 * (y * y * y)))
    cdf = 0.5 * (1.0 + t)
    slope = cdf + 0.5 * y * (1.0 - t * t) * (c * (1.0 + 3.0 * 0.044715 * (y * y)))
    return y * cdf, slope


def kernel(
    act_ref,
    basis_ref,
    depth_ref,
    extent_ref,
    w1_ref,
    w2_ref,
    cot_ref,
    out_ref,
    gfield_ref,
    g1_ref,
    g2_ref,
    basis,
    depth,
    extent,
    cot,
    pad,
    cb,
    t1,
    tfwd,
    tadj,
    first,
    xs,
    wl,
    wf,
    zb,
    zw,
    xt,
    xg,
    zg,
    sg,
    pb,
    ry,
    qy,
    rz,
    fin,
    yb,
    send_sem,
    recv_sem,
    load_sem,
):
    lat = lax.axis_index("lat")
    lon = lax.axis_index("lon")
    z, core = lat // 2, lat % 2
    x, y = lon // NY, lon % NY
    other = 1 - core
    sib = lat + 1 - 2 * core

    def at_x(d):
        return lax.rem(x + d, NX) * NY + y

    def at_y(d):
        return x * NY + lax.rem(y + d, NY)

    def at_z(d):
        return lax.rem(z + d, NZ) * 2 + core

    n_lat, n_lon = 2 * NZ, NX * NY
    lat_up, lat_dn = lax.rem(lat + n_lat - 1, n_lat), lax.rem(lat + 1, n_lat)

    def at_lon(d):
        return lax.rem(lon + d + n_lon, n_lon)

    lon_lf, lon_rt = at_lon(-1), at_lon(1)

    barrier = pltpu.get_barrier_semaphore()
    peers = [(sib, lon)]
    peers += [(lat, at_x(d)) for d in range(1, NX)] + [(sib, at_x(d)) for d in range(1, NX)]
    peers += [(lat, at_y(d)) for d in range(1, NY)] + [(at_z(d), lon) for d in range(1, NZ)]
    peers += [(a, at_lon(d)) for a in (lat_up, lat_dn) for d in (-2, -1, 0, 1, 2)]
    peers += [(lat, at_lon(d)) for d in (-2, -1, 1, 2)]
    for peer in peers:
        pl.semaphore_signal(barrier, inc=1, device_id=peer, device_id_type=pl.DeviceIdType.MESH)

    half = pl.ds(pl.multiple_of(core * 128, 128), 128)
    loads = []

    def load(src, dst):
        copy = pltpu.make_async_copy(src, dst, load_sem.at[len(loads)])
        copy.start()
        loads.append(copy)

    load(w1_ref.at[:, :, half], wl.at[0, core, x, y])
    load(act_ref, first.at[SIDE + OWN : SIDE + OWN + CELLS])
    load(basis_ref, basis)
    load(depth_ref, depth)
    load(extent_ref, extent)
    load(w2_ref.at[:, :, half], wl.at[1, core, x, y])
    load(cot_ref, cot)

    sent = []

    def send(copies, whole):
        slot = len(sent)

        def describe(src, dst, device):
            return pltpu.make_async_remote_copy(
                src_ref=src,
                dst_ref=dst,
                send_sem=send_sem.at[slot],
                recv_sem=recv_sem.at[slot],
                device_id=device,
                device_id_type=pl.DeviceIdType.MESH,
            )

        for src, dst, device in copies:
            describe(src, dst, device).start()
        group = describe(whole, whole, (sib, lon))
        sent.append(group)
        return group

    def arrive(*groups):
        for copy in groups:
            copy.wait_recv()

    first[5 * SIDE : FIRST, :] = jnp.zeros((FIRST - 5 * SIDE, CH), BF16)
    for side in range(3):
        for edge in (side * SIDE, side * SIDE + SIDE - 16):
            xs[:, edge : edge + 16, :] = jnp.zeros((3, 16, CH), BF16)
    xs[:, 3 * SIDE : EXT, :] = jnp.zeros((3, EXT - 3 * SIDE, CH), BF16)
    loads[0].wait()
    loads[1].wait()
    pl.semaphore_wait(barrier, len(peers))

    def halo(field):
        n = field - 1
        own = xs.at[n, OWN : OWN + CELLS]
        top = xs.at[n, OWN : OWN + 16]
        bottom = xs.at[n, OWN + CELLS - 16 : OWN + CELLS]
        lf, mid, rt = 0, SIDE, 2 * SIDE
        low, high = 32, SIDE - 32

        def to(src, base, off, rows, device):
            return src, xs.at[n, base + off : base + off + rows], device

        return send(
            [
                to(own, lf, low, CELLS, (lat, lon_rt)),
                to(own, rt, low, CELLS, (lat, lon_lf)),
                to(bottom, lf, 16, 16, (lat_dn, lon_rt)),
                to(bottom, rt, 16, 16, (lat_dn, lon_lf)),
                to(top, lf, high, 16, (lat_up, lon_rt)),
                to(top, rt, high, 16, (lat_up, lon_lf)),
                to(bottom, mid, 16, 16, (lat_dn, lon)),
                to(top, mid, high, 16, (lat_up, lon)),
            ],
            xs.at[n, 0 : 2 * CELLS + 6 * 16],
        )

    def wide_halo():
        base = SIDE + OWN
        own = first.at[base : base + CELLS]
        top, bottom = first.at[base : base + 32], first.at[base + CELLS - 32 : base + CELLS]
        copies = []
        for d in (-1, 1, -2, 2, 0):
            at = (2 - d) * SIDE
            copies.append((bottom, first.at[at : at + 32], (lat_dn, at_lon(d))))
            copies.append((top, first.at[at + SIDE - 32 : at + SIDE], (lat_up, at_lon(d))))
            if d:
                copies.append((own, first.at[at + 32 : at + 32 + CELLS], (lat, at_lon(d))))
        return send(copies, first.at[0 : 4 * CELLS + 10 * 32])

    def gather(w):
        ka, kc = slice(0, SPLIT), slice(SPLIT, BASIS)
        mine_a, mine_c = wl.at[w, core, x, y, ka], wl.at[w, core, x, y, kc]
        first_c = send(
            [(mine_c, mine_c, (lat, at_y(d))) for d in range(1, NY)], wl.at[w, core, x, 0 : NY - 1, kc]
        )
        first_a = send(
            [(mine_a, mine_a, (lat, at_x(d))) for d in range(1, NX)], wl.at[w, core, 0 : NX - 1, y, ka]
        )
        yield
        arrive(first_a)
        column = wl.at[w, core, :, y, ka]
        second_a = send(
            [(column, column, (lat, at_y(d))) for d in range(1, NY)], wl.at[w, core, :, 0 : NY - 1, ka]
        )
        arrive(first_c)

        def row(d):
            return wl.at[w, core, lax.rem(x + d, NX), :, kc]

        second_c = [send([(row(0), row(0), (lat, at_x(d)))], row(0)) for d in range(1, NX)]
        shared = []

        def share(ref):
            shared.append(send([(ref, ref, (sib, lon))], ref))

        share(row(0))
        yield
        for d in (1, 3, 2):
            arrive(second_c[d - 1])
            share(row(NX - d))
        arrive(second_a)
        share(wl.at[w, core, :, :, ka])
        yield
        arrive(*shared)

    gather1, gather2 = gather(0), gather(1)
    next(gather1)
    in_halo = wide_halo()
    loads[5].wait()
    next(gather2)

    for copy in loads[2:5]:
        copy.wait()
    sub = lax.broadcasted_iota(jnp.int32, (8, 128), 0)
    lane = lax.broadcasted_iota(jnp.int32, (8, 128), 1)
    slot_a = (lane * 2731) >> 16
    slot_b = lane - 24 * slot_a
    row0 = lat * ROWS
    picks = 8 * (ROWS + 4)
    pick_row = lax.broadcasted_iota(jnp.int32, (picks, GRID), 0) >> 3
    pick_lane = lax.broadcasted_iota(jnp.int32, (picks, GRID), 1)
    pick = jnp.where(pick_lane == pick_row + row0 - 2, 1.0, 0.0).astype(BF16)
    for k in range(BASIS):
        for a in range(5):
            pad[k, 24 * a : 24 * a + 17, :] = basis[k, a].astype(F32)
        picked = lax.dot_general(
            pick, pad[k].astype(BF16), (((1,), (1,)), ((), ())), preferred_element_type=F32
        )
        cb[:, k] = picked.reshape(ROWS + 4, 8, 128)

    def coef_row(r, carry):
        wrapped = lax.rem(row0 + r + GRID - 2, GRID)
        inside = (
            (jnp.abs(slot_a - 2) <= depth[wrapped])
            & (jnp.abs(slot_b - 8) <= extent[wrapped])
            & (slot_a < 5)
        )
        for k in range(BASIS):
            cb[r, k] = jnp.where(inside, cb[r, k], 0.0)
        return carry

    lax.fori_loop(0, ROWS + 4, coef_row, 0)

    wide_l = lax.broadcasted_iota(jnp.int32, (256, EXT), 0)
    wide_t = lax.broadcasted_iota(jnp.int32, (256, EXT), 1)
    l_q = wide_l >> 7
    l_in = wide_l & 127
    l_a = (l_in * 2731) >> 16
    l_m = l_in - 24 * l_a

    def build(n):
        def pair(p, carry):
            for q in range(2):
                i = 2 * p + q
                row = row0 + i - 2
                for k in range(BASIS):
                    if n == 0:
                        reach = row + slot_a - 2
                        tile = jnp.where((reach >= 0) & (reach < GRID), cb[i, k], 0.0)
                        tile = pltpu.roll(tile, 0, 1, stride=1, stride_axis=0)
                    else:
                        tile = cb[i + 4, k]
                        for a in range(1, 5):
                            tile = jnp.where(slot_a == a, cb[i + 4 - a, k], tile)
                        tile = pltpu.roll(tile, 0, 1, stride=1, stride_axis=0)
                    t1[p, k, 8 * q : 8 * q + 8, 128 * q : 128 * q + 128] = tile
                    t1[p, k, 8 * q : 8 * q + 8, 128 * (1 - q) : 128 * (1 - q) + 128] = jnp.zeros(
                        (8, 128), F32
                    )
            return carry

        if n == 1:
            src = lax.broadcasted_iota(jnp.int32, (128, 128), 0)
            dst = lax.broadcasted_iota(jnp.int32, (128, 128), 1)
            src_a = (src * 2731) >> 16
            mirror = jnp.where(
                (dst == 48 * src_a + 16 - src) & (src - 24 * src_a < 17) & (src_a < 5), 1.0, 0.0
            ).astype(BF16)
            for r in range(0, ROWS + 4, 4):
                rows = cb[r : r + 4].reshape(4 * BASIS * 8, 128).astype(BF16)
                cb[r : r + 4] = jnp.dot(rows, mirror, preferred_element_type=F32).reshape(
                    4, BASIS, 8, 128
                )
        pairs = 8 if n else 10
        lax.fori_loop(0, pairs, pair, 0)
        m = l_m
        shift = l_q + (l_a if n == 0 else 6 - l_a)
        place = jnp.where(
            (wide_t == (m >> 3) * SIDE + 8 * shift + (m & 7)) & (l_a < 5), 1.0, 0.0
        ).astype(BF16)
        for p in range(pairs):
            spread = jnp.dot(
                t1[p].reshape(16 * BASIS, 256).astype(BF16), place, preferred_element_type=F32
            )
            spread = pltpu.roll(spread, 16 * p, 1) if p else spread
            (tadj if n else tfwd)[:, 16 * p : 16 * p + 16, :] = spread.reshape(BASIS, 16, EXT).astype(BF16)

    build(0)

    def conv(n, field):
        for k in range(0, BASIS, 3):
            maps = tadj[k : k + 3] if n else tfwd[k : k + 3, 16 : 16 + CELLS]
            part = jnp.dot(
                maps.reshape(3 * CELLS, EXT), xs[field - 1], preferred_element_type=F32
            )
            zb[k : k + 3] = part.astype(BF16).reshape(3, CELLS, CH)

    def conv_wide():
        for side in range(3):
            for k in range(0, BASIS, 3):
                part = jnp.dot(
                    tfwd[k : k + 3].reshape(3 * WIDE, EXT),
                    first[SIDE * side : SIDE * side + EXT],
                    preferred_element_type=F32,
                )
                zw[side, k : k + 3] = part.astype(BF16).reshape(3, WIDE, CH)

    def mix_wide(side):
        total = jnp.zeros((WIDE, CH), F32)
        for k in range(BASIS):
            total += jnp.dot(zw[side, k], wf[0, k], preferred_element_type=F32)
        at = SIDE * (side + 1) + 16
        base = first[at : at + WIDE, :].astype(F32)
        at = SIDE * side + 16
        xs[0, at : at + WIDE, :] = (base + gelu_and_slope(total)[0]).astype(BF16)
        if side == 1:
            yb[...] = total[16 : 16 + CELLS]

    def spread_x(layer):
        field = xs[0] if layer else first[SIDE : SIDE + EXT]
        xt[layer] = field.astype(F32).T.astype(BF16)
        xg[layer, x] = xt[layer, pl.ds(pl.multiple_of(x * 64, 64), 64)]

        def block(d):
            return xt.at[layer, pl.ds(pl.multiple_of(lax.rem(x + d, NX) * 64, 64), 64)]

        got = send(
            [(block(d), xg.at[layer, x], (lat, at_x(d))) for d in (2, 1, 3)],
            xg.at[layer, 0 : NX - 1],
        )
        yield
        arrive(got)
        for k in range(0, BASIS, 3):
            part = lax.dot_general(
                xg[layer].reshape(NX * 64, EXT),
                tfwd[k : k + 3, 16 : 16 + CELLS].reshape(3 * CELLS, EXT),
                (((1,), (1,)), ((), ())),
                preferred_element_type=F32,
            ).astype(BF16)
            for a in range(NX):
                for b in range(3):
                    zg[layer, a, core, k + b] = part[
                        64 * a : 64 * a + 64, CELLS * b : CELLS * b + CELLS
                    ]
        mine = zg.at[layer, :, core]
        shared = send([(mine, mine, (sib, lon))], mine)
        yield
        arrive(shared)

    def settle(w):
        for k in range(BASIS):
            for h in range(2):
                wf[w, k, :, h * 128 : (h + 1) * 128] = (
                    wl[w, h, :, :, k].astype(F32).reshape(CH, 128).astype(BF16)
                )

    def mix(w):
        total = jnp.zeros((CELLS, CH), F32)
        for k in range(BASIS):
            total += jnp.dot(zb[k], wf[w, k], preferred_element_type=F32)
        return total

    def mix_back(w):
        total = jnp.zeros((CELLS, CH), F32)
        for k in range(BASIS):
            total += lax.dot_general(
                zb[k], wf[w, k], (((1,), (1,)), ((), ())), preferred_element_type=F32
            )
        return total

    def own_block(n):
        return xs[n - 1, OWN : OWN + CELLS, :].astype(F32)

    def spread_s(layer, n, values):
        xs[n - 1, OWN : OWN + CELLS, :] = values
        if layer:
            around = halo(n)
        for h in range(2):

            @pl.when(core == h)
            def _():
                sg[layer, x, h] = values[:, h * 128 : (h + 1) * 128]

        copies = []
        for d in (1, 3, 2, 0):
            for dc in range(2):
                if d == 0 and dc == 0:
                    continue
                h = core if dc == 0 else other
                src = xs.at[n - 1, OWN : OWN + CELLS, pl.ds(pl.multiple_of(h * 128, 128), 128)]
                copies.append((src, sg.at[layer, x, core], (lat if dc == 0 else sib, at_x(d))))
        spread = send(copies, xs.at[n - 1, 0 : 7 * CELLS // 2])
        if not layer:
            around = halo(n)
        return around, spread

    def weight_partial(layer):
        groups = []
        for c in range(PARTS):
            total = jnp.zeros((DEEP * 64, 128), F32)
            ks = slice(DEEP * c, DEEP * c + DEEP)
            for a in range(NX):
                left = jnp.concatenate(
                    [zg[layer, a, h, ks].reshape(DEEP * 64, 128) for h in range(2)], axis=1
                )
                total += jnp.dot(left, sg[layer, a].reshape(256, 128), preferred_element_type=F32)
            blocks = total.reshape(DEEP, NY, 8, 128)
            for b in range(NY):
                pb[layer, c, b] = blocks[:, b].astype(BF16)
            ry[layer, c, y] = pb[layer, c, y]
            groups.append(
                send(
                    [
                        (pb.at[layer, c, lax.rem(y + d, NY)], ry.at[layer, c, y], (lat, at_y(d)))
                        for d in (4, 3, 5, 2, 6, 1, 7)
                    ],
                    ry.at[layer, c, 0 : NY - 1],
                )
            )
        return groups

    def weight_rows(layer, got):
        groups = []
        for c in range(PARTS):
            arrive(got[c])
            qy[layer, c] = jnp.sum(ry[layer, c].astype(F32), axis=0).astype(BF16)
            rz[layer, c, z] = qy[layer, c]
            groups.append(
                send(
                    [
                        (qy.at[layer, c], rz.at[layer, c, z], (at_z(d), lon))
                        for d in (4, 3, 5, 2, 6, 1, 7)
                    ],
                    rz.at[layer, c, 0 : NZ - 1],
                )
            )
        return groups

    def weight_bands(layer, got):
        groups = []
        for c in range(PARTS):
            arrive(got[c])
            ks = slice(DEEP * c, DEEP * c + DEEP)
            fin[layer, core, ks] = jnp.sum(rz[layer, c].astype(F32), axis=0)
            mine = fin.at[layer, core, ks]
            groups.append(send([(mine, mine, (sib, lon))], mine))
        return groups

    next(gather1)
    build(1)
    next(gather2)
    arrive(in_halo)
    conv_wide()
    z1 = spread_x(0)
    next(z1)
    next(gather1)
    next(gather1, None)
    settle(0)
    for side in range(3):
        mix_wide(side)
    next(gather2)
    z2 = spread_x(1)
    next(z2)
    conv(0, 1)
    next(gather2, None)
    settle(1)
    y2 = mix(1)
    grown, slope = gelu_and_slope(y2)
    loads[6].wait()
    around2, all_s2 = spread_s(1, 2, (cot[...].astype(F32) * slope).astype(BF16))
    out_ref[...] = (own_block(1) + grown).astype(BF16)
    next(z1)
    next(z2)
    arrive(around2)
    conv(1, 2)
    grad_hidden = (cot[...].astype(F32) + mix_back(1)).astype(BF16).astype(F32)
    s1 = (grad_hidden * gelu_and_slope(yb[...])[1]).astype(BF16)
    around1, all_s1 = spread_s(0, 3, s1)
    arrive(all_s2)
    next(z2, None)
    p2 = weight_partial(1)
    next(z1, None)
    arrive(all_s1)
    p1 = weight_partial(0)
    arrive(around1)
    conv(1, 3)
    q2 = weight_rows(1, p2)
    gfield_ref[...] = (grad_hidden + mix_back(0)).astype(BF16)
    q1 = weight_rows(0, p1)
    r2 = weight_bands(1, q2)
    r1 = weight_bands(0, q1)
    for layer, ref, got in ((1, g2_ref, r2), (0, g1_ref, r1)):
        for group in got:
            arrive(group)
        for h in range(2):
            ref[:, :, h * 128 : (h + 1) * 128] = fin[layer, h]
    for copy in sent:
        copy.wait_send()


def deliver(*refs):
    count = len(refs) // 2
    for src, dst in zip(refs[:count], refs[count:]):
        dst[...] = src[...]


def local(activation, basis_table, lat_depth, lon_extent, weight_one, weight_two, cotangent):
    vmem = pl.BlockSpec(memory_space=pltpu.VMEM)
    hbm = pl.BlockSpec(memory_space=pltpu.HBM)
    field = jax.ShapeDtypeStruct((CELLS, CH), BF16)
    grad = jax.ShapeDtypeStruct((BASIS, 8, CH), F32)
    shapes = (field, field, grad, grad)
    results = pl.pallas_call(
        kernel,
        out_shape=shapes,
        in_specs=[hbm] * 7,
        out_specs=(vmem,) * 4,
        scratch_shapes=[
            pltpu.VMEM((BASIS, 5, 17, GRID), BF16),
            pltpu.SMEM((GRID,), jnp.int32),
            pltpu.SMEM((GRID,), jnp.int32),
            pltpu.VMEM((CELLS, CH), BF16),
            pltpu.VMEM((BASIS, 128, GRID), F32),
            pltpu.VMEM((ROWS + 4, BASIS, 8, 128), F32),
            pltpu.VMEM((10, BASIS, 16, 256), F32),
            pltpu.VMEM((BASIS, WIDE, EXT), BF16),
            pltpu.VMEM((BASIS, CELLS, EXT), BF16),
            pltpu.VMEM((FIRST, CH), BF16),
            pltpu.VMEM((3, EXT, CH), BF16),
            pltpu.VMEM((2, 2, NX, NY, BASIS, 8, 128), BF16),
            pltpu.VMEM((2, BASIS, CH, CH), BF16),
            pltpu.VMEM((BASIS, CELLS, CH), BF16),
            pltpu.VMEM((3, BASIS, WIDE, CH), BF16),
            pltpu.VMEM((2, CH, EXT), BF16),
            pltpu.VMEM((2, NX, 64, EXT), BF16),
            pltpu.VMEM((2, NX, 2, BASIS, 64, CELLS), BF16),
            pltpu.VMEM((2, NX, 2, CELLS, 128), BF16),
            pltpu.VMEM((2, PARTS, NY, DEEP, 8, 128), BF16),
            pltpu.VMEM((2, PARTS, NY, DEEP, 8, 128), BF16),
            pltpu.VMEM((2, PARTS, DEEP, 8, 128), BF16),
            pltpu.VMEM((2, PARTS, NZ, DEEP, 8, 128), BF16),
            pltpu.VMEM((2, 2, BASIS, 8, 128), F32),
            pltpu.VMEM((CELLS, CH), F32),
            pltpu.SemaphoreType.DMA((SLOTS,)),
            pltpu.SemaphoreType.DMA((SLOTS,)),
            pltpu.SemaphoreType.DMA((7,)),
        ],
        compiler_params=pltpu.CompilerParams(
            collective_id=0, has_side_effects=True, vmem_limit_bytes=63 * 1024 * 1024
        ),
        cost_estimate=pl.CostEstimate(flops=10**9, bytes_accessed=10**7, transcendentals=10**5),
    )(
        activation.reshape(CELLS, CH),
        jnp.transpose(basis_table, (0, 2, 3, 1)),
        lat_depth,
        lon_extent,
        weight_one,
        weight_two,
        cotangent.reshape(CELLS, CH),
    )
    out, grad_field, grad_one, grad_two = pl.pallas_call(
        deliver,
        out_shape=shapes,
        in_specs=[vmem] * 4,
        out_specs=(vmem,) * 4,
    )(*results)
    block = (ROWS, COLS, CH)
    return out.reshape(block), grad_field.reshape(block), grad_one, grad_two


def solution(mesh):
    field = P("lat", "lon", None)
    weight = P(None, "lon", None)
    return jax.shard_map(
        local,
        mesh=mesh,
        in_specs=(field, P(), P(), P(), weight, weight, field),
        out_specs=(field, field, weight, weight),
        check_vma=False,
    )
```

```python
import jax
import jax.numpy as jnp
from jax import lax
from jax.experimental import pallas as pl
from jax.experimental.pallas import tpu as pltpu
from jax.sharding import PartitionSpec as P

NX, NY, NZ = 4, 8, 8
BASIS = 9
CH = 256
ROWS, COLS = 16, 8
CELLS = ROWS * COLS
GRID = 256
SIDE = (ROWS + 4) * COLS
EXT = 512
OWN = SIDE + 2 * COLS
F32 = jnp.float32
BF16 = jnp.bfloat16
SLOTS = 60
SPLIT = 2
PARTS, DEEP = 3, 3


def gelu_and_slope(y):
    c = 0.7978845608028654
    t = jnp.tanh(c * (y + 0.044715 * (y * y * y)))
    cdf = 0.5 * (1.0 + t)
    slope = cdf + 0.5 * y * (1.0 - t * t) * (c * (1.0 + 3.0 * 0.044715 * (y * y)))
    return y * cdf, slope


def kernel(
    act_ref,
    basis_ref,
    depth_ref,
    extent_ref,
    w1_ref,
    w2_ref,
    cot_ref,
    out_ref,
    gfield_ref,
    g1_ref,
    g2_ref,
    basis,
    depth,
    extent,
    cot,
    pad,
    cb,
    t1,
    tmap,
    xs,
    wl,
    wf,
    zb,
    xt,
    xg,
    zg,
    sg,
    pb,
    ry,
    qy,
    rz,
    fin,
    yb,
    send_sem,
    recv_sem,
    load_sem,
):
    lat = lax.axis_index("lat")
    lon = lax.axis_index("lon")
    z, core = lat // 2, lat % 2
    x, y = lon // NY, lon % NY
    other = 1 - core
    sib = lat + 1 - 2 * core

    def at_x(d):
        return lax.rem(x + d, NX) * NY + y

    def at_y(d):
        return x * NY + lax.rem(y + d, NY)

    def at_z(d):
        return lax.rem(z + d, NZ) * 2 + core

    n_lat, n_lon = 2 * NZ, NX * NY
    lat_up, lat_dn = lax.rem(lat + n_lat - 1, n_lat), lax.rem(lat + 1, n_lat)
    lon_lf, lon_rt = lax.rem(lon + n_lon - 1, n_lon), lax.rem(lon + 1, n_lon)

    barrier = pltpu.get_barrier_semaphore()
    peers = [(sib, lon)]
    peers += [(lat, at_x(d)) for d in range(1, NX)] + [(sib, at_x(d)) for d in range(1, NX)]
    peers += [(lat, at_y(d)) for d in range(1, NY)] + [(at_z(d), lon) for d in range(1, NZ)]
    peers += [
        (a, b)
        for a in (lat_up, lat, lat_dn)
        for b in (lon_lf, lon, lon_rt)
        if not (a is lat and b is lon)
    ]
    for peer in peers:
        pl.semaphore_signal(barrier, inc=1, device_id=peer, device_id_type=pl.DeviceIdType.MESH)

    half = pl.ds(pl.multiple_of(core * 128, 128), 128)
    loads = []

    def load(src, dst):
        copy = pltpu.make_async_copy(src, dst, load_sem.at[len(loads)])
        copy.start()
        loads.append(copy)

    load(w1_ref.at[:, :, half], wl.at[0, core, x, y])
    load(act_ref, xs.at[0, OWN : OWN + CELLS])
    load(basis_ref, basis)
    load(depth_ref, depth)
    load(extent_ref, extent)
    load(w2_ref.at[:, :, half], wl.at[1, core, x, y])
    load(cot_ref, cot)

    sent = []

    def send(copies, whole):
        slot = len(sent)

        def describe(src, dst, device):
            return pltpu.make_async_remote_copy(
                src_ref=src,
                dst_ref=dst,
                send_sem=send_sem.at[slot],
                recv_sem=recv_sem.at[slot],
                device_id=device,
                device_id_type=pl.DeviceIdType.MESH,
            )

        for src, dst, device in copies:
            describe(src, dst, device).start()
        group = describe(whole, whole, (sib, lon))
        sent.append(group)
        return group

    def arrive(*groups):
        for copy in groups:
            copy.wait_recv()

    xs[:, 3 * SIDE : EXT, :] = jnp.zeros((4, EXT - 3 * SIDE, CH), BF16)
    loads[0].wait()
    loads[1].wait()
    pl.semaphore_wait(barrier, len(peers))

    def halo(n):
        own = xs.at[n, OWN : OWN + CELLS]
        top = xs.at[n, OWN : OWN + 16]
        bottom = xs.at[n, OWN + CELLS - 16 : OWN + CELLS]
        lf, mid, rt = 0, SIDE, 2 * SIDE
        low, high = 16, SIDE - 16

        def to(src, base, off, rows, device):
            return src, xs.at[n, base + off : base + off + rows], device

        return send(
            [
                to(own, lf, low, CELLS, (lat, lon_rt)),
                to(own, rt, low, CELLS, (lat, lon_lf)),
                to(bottom, lf, 0, 16, (lat_dn, lon_rt)),
                to(bottom, rt, 0, 16, (lat_dn, lon_lf)),
                to(top, lf, high, 16, (lat_up, lon_rt)),
                to(top, rt, high, 16, (lat_up, lon_lf)),
                to(bottom, mid, 0, 16, (lat_dn, lon)),
                to(top, mid, high, 16, (lat_up, lon)),
            ],
            xs.at[n, 0 : 2 * CELLS + 6 * 16],
        )

    def gather(w):
        ka, kc = slice(0, SPLIT), slice(SPLIT, BASIS)
        mine_a, mine_c = wl.at[w, core, x, y, ka], wl.at[w, core, x, y, kc]
        first_c = send(
            [(mine_c, mine_c, (lat, at_y(d))) for d in range(1, NY)], wl.at[w, core, x, 0 : NY - 1, kc]
        )
        first_a = send(
            [(mine_a, mine_a, (lat, at_x(d))) for d in range(1, NX)], wl.at[w, core, 0 : NX - 1, y, ka]
        )
        yield
        arrive(first_a)
        column = wl.at[w, core, :, y, ka]
        second_a = send(
            [(column, column, (lat, at_y(d))) for d in range(1, NY)], wl.at[w, core, :, 0 : NY - 1, ka]
        )
        arrive(first_c)

        def row(d):
            return wl.at[w, core, lax.rem(x + d, NX), :, kc]

        second_c = [send([(row(0), row(0), (lat, at_x(d)))], row(0)) for d in range(1, NX)]
        shared = []

        def share(ref):
            shared.append(send([(ref, ref, (sib, lon))], ref))

        share(row(0))
        yield
        for d in (1, 3, 2):
            arrive(second_c[d - 1])
            share(row(NX - d))
        arrive(second_a)
        share(wl.at[w, core, :, :, ka])
        yield
        arrive(*shared)

    gather1, gather2 = gather(0), gather(1)
    next(gather1)
    in_halo = halo(0)
    loads[5].wait()
    next(gather2)

    for copy in loads[2:5]:
        copy.wait()
    sub = lax.broadcasted_iota(jnp.int32, (8, 128), 0)
    lane = lax.broadcasted_iota(jnp.int32, (8, 128), 1)
    slot_a = (lane * 2731) >> 16
    slot_b = lane - 24 * slot_a
    row0 = lat * ROWS
    picks = 8 * (ROWS + 4)
    pick_row = lax.broadcasted_iota(jnp.int32, (picks, GRID), 0) >> 3
    pick_lane = lax.broadcasted_iota(jnp.int32, (picks, GRID), 1)
    pick = jnp.where(pick_lane == pick_row + row0 - 2, 1.0, 0.0).astype(BF16)
    for k in range(BASIS):
        for a in range(5):
            pad[k, 24 * a : 24 * a + 17, :] = basis[k, a].astype(F32)
        picked = lax.dot_general(
            pick, pad[k].astype(BF16), (((1,), (1,)), ((), ())), preferred_element_type=F32
        )
        cb[:, k] = picked.reshape(ROWS + 4, 8, 128)

    def coef_row(r, carry):
        wrapped = lax.rem(row0 + r + GRID - 2, GRID)
        inside = (
            (jnp.abs(slot_a - 2) <= depth[wrapped])
            & (jnp.abs(slot_b - 8) <= extent[wrapped])
            & (slot_a < 5)
        )
        for k in range(BASIS):
            cb[r, k] = jnp.where(inside, cb[r, k], 0.0)
        return carry

    lax.fori_loop(0, ROWS + 4, coef_row, 0)

    wide_l = lax.broadcasted_iota(jnp.int32, (256, EXT), 0)
    wide_t = lax.broadcasted_iota(jnp.int32, (256, EXT), 1)
    l_q = wide_l >> 7
    l_in = wide_l & 127
    l_a = (l_in * 2731) >> 16
    l_m = l_in - 24 * l_a

    def build(n):
        def pair(p, carry):
            for q in range(2):
                i = 2 * p + q
                row = row0 + i
                for k in range(BASIS):
                    if n == 0:
                        reach = row + slot_a - 2
                        tile = jnp.where((reach >= 0) & (reach < GRID), cb[i + 2, k], 0.0)
                        tile = pltpu.roll(tile, 0, 1, stride=1, stride_axis=0)
                    else:
                        tile = cb[i + 4, k]
                        for a in range(1, 5):
                            tile = jnp.where(slot_a == a, cb[i + 4 - a, k], tile)
                        tile = pltpu.roll(tile, 0, 1, stride=1, stride_axis=0)
                    t1[p, k, 8 * q : 8 * q + 8, 128 * q : 128 * q + 128] = tile
                    t1[p, k, 8 * q : 8 * q + 8, 128 * (1 - q) : 128 * (1 - q) + 128] = jnp.zeros(
                        (8, 128), F32
                    )
            return carry

        if n == 1:
            src = lax.broadcasted_iota(jnp.int32, (128, 128), 0)
            dst = lax.broadcasted_iota(jnp.int32, (128, 128), 1)
            src_a = (src * 2731) >> 16
            mirror = jnp.where(
                (dst == 48 * src_a + 16 - src) & (src - 24 * src_a < 17) & (src_a < 5), 1.0, 0.0
            ).astype(BF16)
            for r in range(0, ROWS + 4, 4):
                rows = cb[r : r + 4].reshape(4 * BASIS * 8, 128).astype(BF16)
                cb[r : r + 4] = jnp.dot(rows, mirror, preferred_element_type=F32).reshape(
                    4, BASIS, 8, 128
                )
        lax.fori_loop(0, 8, pair, 0)
        m = l_m
        shift = l_q + (l_a if n == 0 else 4 - l_a)
        place = jnp.where(
            (wide_t == (m >> 3) * SIDE + 8 * shift + (m & 7)) & (l_a < 5), 1.0, 0.0
        ).astype(BF16)
        for p in range(8):
            spread = jnp.dot(
                t1[p].reshape(16 * BASIS, 256).astype(BF16), place, preferred_element_type=F32
            )
            spread = pltpu.roll(spread, 16 * p, 1) if p else spread
            tmap[n, :, 16 * p : 16 * p + 16, :] = spread.reshape(BASIS, 16, EXT).astype(BF16)

    build(0)

    def conv(n, field):
        for k in range(0, BASIS, 3):
            part = jnp.dot(
                tmap[n, k : k + 3].reshape(3 * CELLS, EXT), xs[field], preferred_element_type=F32
            )
            zb[k : k + 3] = part.astype(BF16).reshape(3, CELLS, CH)

    def spread_x(layer):
        xt[layer] = xs[layer].astype(F32).T.astype(BF16)
        xg[layer, x] = xt[layer, pl.ds(pl.multiple_of(x * 64, 64), 64)]

        def block(d):
            return xt.at[layer, pl.ds(pl.multiple_of(lax.rem(x + d, NX) * 64, 64), 64)]

        got = send(
            [(block(d), xg.at[layer, x], (lat, at_x(d))) for d in (2, 1, 3)],
            xg.at[layer, 0 : NX - 1],
        )
        yield
        arrive(got)
        for k in range(0, BASIS, 3):
            part = lax.dot_general(
                xg[layer].reshape(NX * 64, EXT),
                tmap[0, k : k + 3].reshape(3 * CELLS, EXT),
                (((1,), (1,)), ((), ())),
                preferred_element_type=F32,
            ).astype(BF16)
            for a in range(NX):
                for b in range(3):
                    zg[layer, a, core, k + b] = part[
                        64 * a : 64 * a + 64, CELLS * b : CELLS * b + CELLS
                    ]
        mine = zg.at[layer, :, core]
        shared = send([(mine, mine, (sib, lon))], mine)
        yield
        arrive(shared)

    def settle(w):
        for k in range(BASIS):
            for h in range(2):
                wf[w, k, :, h * 128 : (h + 1) * 128] = (
                    wl[w, h, :, :, k].astype(F32).reshape(CH, 128).astype(BF16)
                )

    def mix(w):
        total = jnp.zeros((CELLS, CH), F32)
        for k in range(BASIS):
            total += jnp.dot(zb[k], wf[w, k], preferred_element_type=F32)
        return total

    def mix_back(w):
        total = jnp.zeros((CELLS, CH), F32)
        for k in range(BASIS):
            total += lax.dot_general(
                zb[k], wf[w, k], (((1,), (1,)), ((), ())), preferred_element_type=F32
            )
        return total

    def own_block(n):
        return xs[n, OWN : OWN + CELLS, :].astype(F32)

    def spread_s(layer, n, values):
        xs[n, OWN : OWN + CELLS, :] = values
        if layer:
            around = halo(n)
        for h in range(2):

            @pl.when(core == h)
            def _():
                sg[layer, x, h] = values[:, h * 128 : (h + 1) * 128]

        copies = []
        for d in (1, 3, 2, 0):
            for dc in range(2):
                if d == 0 and dc == 0:
                    continue
                h = core if dc == 0 else other
                src = xs.at[n, OWN : OWN + CELLS, pl.ds(pl.multiple_of(h * 128, 128), 128)]
                copies.append((src, sg.at[layer, x, core], (lat if dc == 0 else sib, at_x(d))))
        spread = send(copies, xs.at[n, 0 : 7 * CELLS // 2])
        if not layer:
            around = halo(n)
        return around, spread

    def weight_partial(layer):
        groups = []
        for c in range(PARTS):
            total = jnp.zeros((DEEP * 64, 128), F32)
            ks = slice(DEEP * c, DEEP * c + DEEP)
            for a in range(NX):
                left = jnp.concatenate(
                    [zg[layer, a, h, ks].reshape(DEEP * 64, 128) for h in range(2)], axis=1
                )
                total += jnp.dot(left, sg[layer, a].reshape(256, 128), preferred_element_type=F32)
            blocks = total.reshape(DEEP, NY, 8, 128)
            for b in range(NY):
                pb[layer, c, b] = blocks[:, b].astype(BF16)
            ry[layer, c, y] = pb[layer, c, y]
            groups.append(
                send(
                    [
                        (pb.at[layer, c, lax.rem(y + d, NY)], ry.at[layer, c, y], (lat, at_y(d)))
                        for d in (4, 3, 5, 2, 6, 1, 7)
                    ],
                    ry.at[layer, c, 0 : NY - 1],
                )
            )
        return groups

    def weight_rows(layer, got):
        groups = []
        for c in range(PARTS):
            arrive(got[c])
            qy[layer, c] = jnp.sum(ry[layer, c].astype(F32), axis=0).astype(BF16)
            rz[layer, c, z] = qy[layer, c]
            groups.append(
                send(
                    [
                        (qy.at[layer, c], rz.at[layer, c, z], (at_z(d), lon))
                        for d in (4, 3, 5, 2, 6, 1, 7)
                    ],
                    rz.at[layer, c, 0 : NZ - 1],
                )
            )
        return groups

    def weight_bands(layer, got):
        groups = []
        for c in range(PARTS):
            arrive(got[c])
            ks = slice(DEEP * c, DEEP * c + DEEP)
            fin[layer, core, ks] = jnp.sum(rz[layer, c].astype(F32), axis=0)
            mine = fin.at[layer, core, ks]
            groups.append(send([(mine, mine, (sib, lon))], mine))
        return groups

    next(gather1)
    build(1)
    next(gather2)
    arrive(in_halo)
    conv(0, 0)
    next(gather1)
    next(gather1, None)
    settle(0)
    y1 = mix(0)
    yb[...] = y1
    hidden = (own_block(0) + gelu_and_slope(y1)[0]).astype(BF16)
    xs[1, OWN : OWN + CELLS, :] = hidden
    mid_halo = halo(1)
    z1 = spread_x(0)
    next(z1)
    next(gather2)
    next(gather2, None)
    settle(1)
    arrive(mid_halo)
    conv(0, 1)
    y2 = mix(1)
    grown, slope = gelu_and_slope(y2)
    loads[6].wait()
    around2, all_s2 = spread_s(1, 2, (cot[...].astype(F32) * slope).astype(BF16))
    z2 = spread_x(1)
    next(z2)
    out_ref[...] = (own_block(1) + grown).astype(BF16)
    next(z1)
    arrive(around2)
    conv(1, 2)
    grad_hidden = (cot[...].astype(F32) + mix_back(1)).astype(BF16).astype(F32)
    s1 = (grad_hidden * gelu_and_slope(yb[...])[1]).astype(BF16)
    around1, all_s1 = spread_s(0, 3, s1)
    next(z2)
    arrive(all_s2)
    next(z1, None)
    next(z2, None)
    p2 = weight_partial(1)
    arrive(all_s1)
    p1 = weight_partial(0)
    arrive(around1)
    conv(1, 3)
    q2 = weight_rows(1, p2)
    gfield_ref[...] = (grad_hidden + mix_back(0)).astype(BF16)
    q1 = weight_rows(0, p1)
    r2 = weight_bands(1, q2)
    r1 = weight_bands(0, q1)
    for layer, ref, got in ((1, g2_ref, r2), (0, g1_ref, r1)):
        for group in got:
            arrive(group)
        for h in range(2):
            ref[:, :, h * 128 : (h + 1) * 128] = fin[layer, h]
    for copy in sent:
        copy.wait_send()


def deliver(*refs):
    count = len(refs) // 2
    for src, dst in zip(refs[:count], refs[count:]):
        dst[...] = src[...]


def local(activation, basis_table, lat_depth, lon_extent, weight_one, weight_two, cotangent):
    vmem = pl.BlockSpec(memory_space=pltpu.VMEM)
    hbm = pl.BlockSpec(memory_space=pltpu.HBM)
    field = jax.ShapeDtypeStruct((CELLS, CH), BF16)
    grad = jax.ShapeDtypeStruct((BASIS, 8, CH), F32)
    shapes = (field, field, grad, grad)
    results = pl.pallas_call(
        kernel,
        out_shape=shapes,
        in_specs=[hbm] * 7,
        out_specs=(vmem,) * 4,
        scratch_shapes=[
            pltpu.VMEM((BASIS, 5, 17, GRID), BF16),
            pltpu.SMEM((GRID,), jnp.int32),
            pltpu.SMEM((GRID,), jnp.int32),
            pltpu.VMEM((CELLS, CH), BF16),
            pltpu.VMEM((BASIS, 128, GRID), F32),
            pltpu.VMEM((ROWS + 4, BASIS, 8, 128), F32),
            pltpu.VMEM((8, BASIS, 16, 256), F32),
            pltpu.VMEM((2, BASIS, CELLS, EXT), BF16),
            pltpu.VMEM((4, EXT, CH), BF16),
            pltpu.VMEM((2, 2, NX, NY, BASIS, 8, 128), BF16),
            pltpu.VMEM((2, BASIS, CH, CH), BF16),
            pltpu.VMEM((BASIS, CELLS, CH), BF16),
            pltpu.VMEM((2, CH, EXT), BF16),
            pltpu.VMEM((2, NX, 64, EXT), BF16),
            pltpu.VMEM((2, NX, 2, BASIS, 64, CELLS), BF16),
            pltpu.VMEM((2, NX, 2, CELLS, 128), BF16),
            pltpu.VMEM((2, PARTS, NY, DEEP, 8, 128), BF16),
            pltpu.VMEM((2, PARTS, NY, DEEP, 8, 128), BF16),
            pltpu.VMEM((2, PARTS, DEEP, 8, 128), BF16),
            pltpu.VMEM((2, PARTS, NZ, DEEP, 8, 128), BF16),
            pltpu.VMEM((2, 2, BASIS, 8, 128), F32),
            pltpu.VMEM((CELLS, CH), F32),
            pltpu.SemaphoreType.DMA((SLOTS,)),
            pltpu.SemaphoreType.DMA((SLOTS,)),
            pltpu.SemaphoreType.DMA((7,)),
        ],
        compiler_params=pltpu.CompilerParams(
            collective_id=0, has_side_effects=True, vmem_limit_bytes=63 * 1024 * 1024
        ),
        cost_estimate=pl.CostEstimate(flops=10**9, bytes_accessed=10**7, transcendentals=10**5),
    )(
        activation.reshape(CELLS, CH),
        jnp.transpose(basis_table, (0, 2, 3, 1)),
        lat_depth,
        lon_extent,
        weight_one,
        weight_two,
        cotangent.reshape(CELLS, CH),
    )
    out, grad_field, grad_one, grad_two = pl.pallas_call(
        deliver,
        out_shape=shapes,
        in_specs=[vmem] * 4,
        out_specs=(vmem,) * 4,
    )(*results)
    block = (ROWS, COLS, CH)
    return out.reshape(block), grad_field.reshape(block), grad_one, grad_two


def solution(mesh):
    field = P("lat", "lon", None)
    weight = P(None, "lon", None)
    return jax.shard_map(
        local,
        mesh=mesh,
        in_specs=(field, P(), P(), P(), weight, weight, field),
        out_specs=(field, field, weight, weight),
        check_vma=False,
    )
```

```python
import jax
import jax.numpy as jnp
from jax import lax
from jax.experimental import pallas as pl
from jax.experimental.pallas import tpu as pltpu
from jax.sharding import PartitionSpec as P

NX, NY, NZ = 4, 8, 8
BASIS = 9
CH = 256
ROWS, COLS = 16, 8
CELLS = ROWS * COLS
GRID = 256
SIDE = (ROWS + 4) * COLS
EXT = 512
OWN = SIDE + 2 * COLS
F32 = jnp.float32
BF16 = jnp.bfloat16
SLOTS = 44
SPLIT = 2
PARTS = (3, 1)


def gelu_and_slope(y):
    c = 0.7978845608028654
    t = jnp.tanh(c * (y + 0.044715 * (y * y * y)))
    cdf = 0.5 * (1.0 + t)
    slope = cdf + 0.5 * y * (1.0 - t * t) * (c * (1.0 + 3.0 * 0.044715 * (y * y)))
    return y * cdf, slope


def kernel(
    act_ref,
    basis_ref,
    depth_ref,
    extent_ref,
    w1_ref,
    w2_ref,
    cot_ref,
    out_ref,
    gfield_ref,
    g1_ref,
    g2_ref,
    basis,
    depth,
    extent,
    cot,
    pad,
    cb,
    t1,
    tmap,
    xs,
    wl,
    wf,
    zb,
    xt,
    xg,
    zg,
    sg,
    pb,
    ry,
    qy,
    rz,
    fin,
    yb,
    send_sem,
    recv_sem,
    load_sem,
):
    lat = lax.axis_index("lat")
    lon = lax.axis_index("lon")
    z, core = lat // 2, lat % 2
    x, y = lon // NY, lon % NY
    other = 1 - core
    sib = lat + 1 - 2 * core

    def at_x(d):
        return lax.rem(x + d, NX) * NY + y

    def at_y(d):
        return x * NY + lax.rem(y + d, NY)

    def at_z(d):
        return lax.rem(z + d, NZ) * 2 + core

    n_lat, n_lon = 2 * NZ, NX * NY
    lat_up, lat_dn = lax.rem(lat + n_lat - 1, n_lat), lax.rem(lat + 1, n_lat)
    lon_lf, lon_rt = lax.rem(lon + n_lon - 1, n_lon), lax.rem(lon + 1, n_lon)

    barrier = pltpu.get_barrier_semaphore()
    peers = [(sib, lon)]
    peers += [(lat, at_x(d)) for d in range(1, NX)] + [(sib, at_x(d)) for d in range(1, NX)]
    peers += [(lat, at_y(d)) for d in range(1, NY)] + [(at_z(d), lon) for d in range(1, NZ)]
    peers += [
        (a, b)
        for a in (lat_up, lat, lat_dn)
        for b in (lon_lf, lon, lon_rt)
        if not (a is lat and b is lon)
    ]
    for peer in peers:
        pl.semaphore_signal(barrier, inc=1, device_id=peer, device_id_type=pl.DeviceIdType.MESH)

    half = pl.ds(pl.multiple_of(core * 128, 128), 128)
    loads = []

    def load(src, dst):
        copy = pltpu.make_async_copy(src, dst, load_sem.at[len(loads)])
        copy.start()
        loads.append(copy)

    load(w1_ref.at[:, :, half], wl.at[0, core, x, y])
    load(act_ref, xs.at[0, OWN : OWN + CELLS])
    load(basis_ref, basis)
    load(depth_ref, depth)
    load(extent_ref, extent)
    load(w2_ref.at[:, :, half], wl.at[1, core, x, y])
    load(cot_ref, cot)

    sent = []

    def send(copies, whole):
        slot = len(sent)

        def describe(src, dst, device):
            return pltpu.make_async_remote_copy(
                src_ref=src,
                dst_ref=dst,
                send_sem=send_sem.at[slot],
                recv_sem=recv_sem.at[slot],
                device_id=device,
                device_id_type=pl.DeviceIdType.MESH,
            )

        for src, dst, device in copies:
            describe(src, dst, device).start()
        group = describe(whole, whole, (sib, lon))
        sent.append(group)
        return group

    def arrive(*groups):
        for copy in groups:
            copy.wait_recv()

    xs[:, 3 * SIDE : EXT, :] = jnp.zeros((4, EXT - 3 * SIDE, CH), BF16)
    loads[0].wait()
    loads[1].wait()
    pl.semaphore_wait(barrier, len(peers))

    def halo(n):
        own = xs.at[n, OWN : OWN + CELLS]
        top = xs.at[n, OWN : OWN + 16]
        bottom = xs.at[n, OWN + CELLS - 16 : OWN + CELLS]
        lf, mid, rt = 0, SIDE, 2 * SIDE
        low, high = 16, SIDE - 16

        def to(src, base, off, rows, device):
            return src, xs.at[n, base + off : base + off + rows], device

        return send(
            [
                to(own, lf, low, CELLS, (lat, lon_rt)),
                to(own, rt, low, CELLS, (lat, lon_lf)),
                to(bottom, lf, 0, 16, (lat_dn, lon_rt)),
                to(bottom, rt, 0, 16, (lat_dn, lon_lf)),
                to(top, lf, high, 16, (lat_up, lon_rt)),
                to(top, rt, high, 16, (lat_up, lon_lf)),
                to(bottom, mid, 0, 16, (lat_dn, lon)),
                to(top, mid, high, 16, (lat_up, lon)),
            ],
            xs.at[n, 0 : 2 * CELLS + 6 * 16],
        )

    def gather(w):
        ka, kc = slice(0, SPLIT), slice(SPLIT, BASIS)
        mine_a, mine_c = wl.at[w, core, x, y, ka], wl.at[w, core, x, y, kc]
        first_c = send(
            [(mine_c, mine_c, (lat, at_y(d))) for d in range(1, NY)], wl.at[w, core, x, 0 : NY - 1, kc]
        )
        first_a = send(
            [(mine_a, mine_a, (lat, at_x(d))) for d in range(1, NX)], wl.at[w, core, 0 : NX - 1, y, ka]
        )
        yield
        arrive(first_a)
        column = wl.at[w, core, :, y, ka]
        second_a = send(
            [(column, column, (lat, at_y(d))) for d in range(1, NY)], wl.at[w, core, :, 0 : NY - 1, ka]
        )
        arrive(first_c)

        def row(d):
            return wl.at[w, core, lax.rem(x + d, NX), :, kc]

        second_c = [send([(row(0), row(0), (lat, at_x(d)))], row(0)) for d in range(1, NX)]
        shared = []

        def share(ref):
            shared.append(send([(ref, ref, (sib, lon))], ref))

        share(row(0))
        yield
        for d in (1, 3, 2):
            arrive(second_c[d - 1])
            share(row(NX - d))
        arrive(second_a)
        share(wl.at[w, core, :, :, ka])
        yield
        arrive(*shared)

    gather1, gather2 = gather(0), gather(1)
    next(gather1)
    in_halo = halo(0)
    loads[5].wait()
    next(gather2)

    for copy in loads[2:5]:
        copy.wait()
    sub = lax.broadcasted_iota(jnp.int32, (8, 128), 0)
    lane = lax.broadcasted_iota(jnp.int32, (8, 128), 1)
    slot_a = (lane * 2731) >> 16
    slot_b = lane - 24 * slot_a
    row0 = lat * ROWS
    picks = 8 * (ROWS + 4)
    pick_row = lax.broadcasted_iota(jnp.int32, (picks, GRID), 0) >> 3
    pick_lane = lax.broadcasted_iota(jnp.int32, (picks, GRID), 1)
    pick = jnp.where(pick_lane == pick_row + row0 - 2, 1.0, 0.0).astype(BF16)
    for k in range(BASIS):
        for a in range(5):
            pad[k, 24 * a : 24 * a + 17, :] = basis[k, a].astype(F32)
        picked = lax.dot_general(
            pick, pad[k].astype(BF16), (((1,), (1,)), ((), ())), preferred_element_type=F32
        )
        cb[:, k] = picked.reshape(ROWS + 4, 8, 128)

    def coef_row(r, carry):
        wrapped = lax.rem(row0 + r + GRID - 2, GRID)
        inside = (
            (jnp.abs(slot_a - 2) <= depth[wrapped])
            & (jnp.abs(slot_b - 8) <= extent[wrapped])
            & (slot_a < 5)
        )
        for k in range(BASIS):
            cb[r, k] = jnp.where(inside, cb[r, k], 0.0)
        return carry

    lax.fori_loop(0, ROWS + 4, coef_row, 0)

    wide_l = lax.broadcasted_iota(jnp.int32, (256, EXT), 0)
    wide_t = lax.broadcasted_iota(jnp.int32, (256, EXT), 1)
    l_q = wide_l >> 7
    l_in = wide_l & 127
    l_a = (l_in * 2731) >> 16
    l_m = l_in - 24 * l_a

    def build(n):
        def pair(p, carry):
            for q in range(2):
                i = 2 * p + q
                row = row0 + i
                for k in range(BASIS):
                    if n == 0:
                        reach = row + slot_a - 2
                        tile = jnp.where((reach >= 0) & (reach < GRID), cb[i + 2, k], 0.0)
                        tile = pltpu.roll(tile, 0, 1, stride=1, stride_axis=0)
                    else:
                        tile = cb[i + 4, k]
                        for a in range(1, 5):
                            tile = jnp.where(slot_a == a, cb[i + 4 - a, k], tile)
                        tile = pltpu.roll(tile, 0, 1, stride=1, stride_axis=0)
                    t1[p, k, 8 * q : 8 * q + 8, 128 * q : 128 * q + 128] = tile
                    t1[p, k, 8 * q : 8 * q + 8, 128 * (1 - q) : 128 * (1 - q) + 128] = jnp.zeros(
                        (8, 128), F32
                    )
            return carry

        if n == 1:
            src = lax.broadcasted_iota(jnp.int32, (128, 128), 0)
            dst = lax.broadcasted_iota(jnp.int32, (128, 128), 1)
            src_a = (src * 2731) >> 16
            mirror = jnp.where(
                (dst == 48 * src_a + 16 - src) & (src - 24 * src_a < 17) & (src_a < 5), 1.0, 0.0
            ).astype(BF16)
            for r in range(0, ROWS + 4, 4):
                rows = cb[r : r + 4].reshape(4 * BASIS * 8, 128).astype(BF16)
                cb[r : r + 4] = jnp.dot(rows, mirror, preferred_element_type=F32).reshape(
                    4, BASIS, 8, 128
                )
        lax.fori_loop(0, 8, pair, 0)
        m = l_m
        shift = l_q + (l_a if n == 0 else 4 - l_a)
        place = jnp.where(
            (wide_t == (m >> 3) * SIDE + 8 * shift + (m & 7)) & (l_a < 5), 1.0, 0.0
        ).astype(BF16)
        for p in range(8):
            spread = jnp.dot(
                t1[p].reshape(16 * BASIS, 256).astype(BF16), place, preferred_element_type=F32
            )
            spread = pltpu.roll(spread, 16 * p, 1) if p else spread
            tmap[n, :, 16 * p : 16 * p + 16, :] = spread.reshape(BASIS, 16, EXT).astype(BF16)

    build(0)

    def conv(n, field):
        for k in range(0, BASIS, 3):
            part = jnp.dot(
                tmap[n, k : k + 3].reshape(3 * CELLS, EXT), xs[field], preferred_element_type=F32
            )
            zb[k : k + 3] = part.astype(BF16).reshape(3, CELLS, CH)

    def spread_x(layer):
        xt[layer] = xs[layer].astype(F32).T.astype(BF16)
        xg[layer, x] = xt[layer, pl.ds(pl.multiple_of(x * 64, 64), 64)]

        def block(d):
            return xt.at[layer, pl.ds(pl.multiple_of(lax.rem(x + d, NX) * 64, 64), 64)]

        got = send(
            [(block(d), xg.at[layer, x], (lat, at_x(d))) for d in (2, 1, 3)],
            xg.at[layer, 0 : NX - 1],
        )
        yield
        arrive(got)
        for k in range(0, BASIS, 3):
            part = lax.dot_general(
                xg[layer].reshape(NX * 64, EXT),
                tmap[0, k : k + 3].reshape(3 * CELLS, EXT),
                (((1,), (1,)), ((), ())),
                preferred_element_type=F32,
            ).astype(BF16)
            for a in range(NX):
                for b in range(3):
                    zg[layer, a, core, k + b] = part[
                        64 * a : 64 * a + 64, CELLS * b : CELLS * b + CELLS
                    ]
        mine = zg.at[layer, :, core]
        shared = send([(mine, mine, (sib, lon))], mine)
        yield
        arrive(shared)

    def settle(w):
        for k in range(BASIS):
            for h in range(2):
                wf[w, k, :, h * 128 : (h + 1) * 128] = (
                    wl[w, h, :, :, k].astype(F32).reshape(CH, 128).astype(BF16)
                )

    def mix(w):
        total = jnp.zeros((CELLS, CH), F32)
        for k in range(BASIS):
            total += jnp.dot(zb[k], wf[w, k], preferred_element_type=F32)
        return total

    def mix_back(w):
        total = jnp.zeros((CELLS, CH), F32)
        for k in range(BASIS):
            total += lax.dot_general(
                zb[k], wf[w, k], (((1,), (1,)), ((), ())), preferred_element_type=F32
            )
        return total

    def own_block(n):
        return xs[n, OWN : OWN + CELLS, :].astype(F32)

    def spread_s(layer, n, values):
        xs[n, OWN : OWN + CELLS, :] = values
        if layer:
            around = halo(n)
        for h in range(2):

            @pl.when(core == h)
            def _():
                sg[layer, x, h] = values[:, h * 128 : (h + 1) * 128]

        copies = []
        for d in (1, 3, 2, 0):
            for dc in range(2):
                if d == 0 and dc == 0:
                    continue
                h = core if dc == 0 else other
                src = xs.at[n, OWN : OWN + CELLS, pl.ds(pl.multiple_of(h * 128, 128), 128)]
                copies.append((src, sg.at[layer, x, core], (lat if dc == 0 else sib, at_x(d))))
        spread = send(copies, xs.at[n, 0 : 7 * CELLS // 2])
        if not layer:
            around = halo(n)
        return around, spread

    def weight_partial(layer):
        groups = []
        deep = BASIS // PARTS[layer]
        for k in range(0, BASIS, deep):
            total = jnp.zeros((deep * 64, 128), F32)
            ks = slice(k, k + deep)
            for a in range(NX):
                left = jnp.concatenate(
                    [zg[layer, a, h, ks].reshape(deep * 64, 128) for h in range(2)], axis=1
                )
                total += jnp.dot(left, sg[layer, a].reshape(256, 128), preferred_element_type=F32)
            blocks = total.reshape(deep, NY, 8, 128)
            for b in range(NY):
                pb[layer, b, ks] = blocks[:, b].astype(BF16)
            ry[layer, y, ks] = pb[layer, y, ks]
            groups.append(
                send(
                    [
                        (pb.at[layer, lax.rem(y + d, NY), ks], ry.at[layer, y, ks], (lat, at_y(d)))
                        for d in (4, 3, 5, 2, 6, 1, 7)
                    ],
                    ry.at[layer, 0 : NY - 1, ks],
                )
            )
        return groups

    def weight_rows(layer, got):
        groups = []
        deep = BASIS // PARTS[layer]
        for c, group in enumerate(got):
            arrive(group)
            ks = slice(deep * c, deep * c + deep)
            qy[layer, ks] = jnp.sum(ry[layer, :, ks].astype(F32), axis=0).astype(BF16)
            rz[layer, z, ks] = qy[layer, ks]
            groups.append(
                send(
                    [
                        (qy.at[layer, ks], rz.at[layer, z, ks], (at_z(d), lon))
                        for d in (4, 3, 5, 2, 6, 1, 7)
                    ],
                    rz.at[layer, 0 : NZ - 1, ks],
                )
            )
        return groups

    def weight_bands(layer, got):
        groups = []
        deep = BASIS // PARTS[layer]
        for c, group in enumerate(got):
            arrive(group)
            ks = slice(deep * c, deep * c + deep)
            fin[layer, core, ks] = jnp.sum(rz[layer, :, ks].astype(F32), axis=0)
            mine = fin.at[layer, core, ks]
            groups.append(send([(mine, mine, (sib, lon))], mine))
        return groups

    next(gather1)
    build(1)
    next(gather2)
    arrive(in_halo)
    conv(0, 0)
    next(gather1)
    next(gather1, None)
    settle(0)
    y1 = mix(0)
    yb[...] = y1
    hidden = (own_block(0) + gelu_and_slope(y1)[0]).astype(BF16)
    xs[1, OWN : OWN + CELLS, :] = hidden
    mid_halo = halo(1)
    z1 = spread_x(0)
    next(z1)
    next(gather2)
    next(gather2, None)
    settle(1)
    arrive(mid_halo)
    conv(0, 1)
    z2 = spread_x(1)
    next(z2)
    y2 = mix(1)
    grown, slope = gelu_and_slope(y2)
    loads[6].wait()
    around2, all_s2 = spread_s(1, 2, (cot[...].astype(F32) * slope).astype(BF16))
    out_ref[...] = (own_block(1) + grown).astype(BF16)
    next(z1)
    next(z2)
    arrive(around2)
    conv(1, 2)
    grad_hidden = (cot[...].astype(F32) + mix_back(1)).astype(BF16).astype(F32)
    s1 = (grad_hidden * gelu_and_slope(yb[...])[1]).astype(BF16)
    around1, all_s1 = spread_s(0, 3, s1)
    arrive(all_s2)
    next(z1, None)
    next(z2, None)
    p2 = weight_partial(1)
    arrive(all_s1)
    p1 = weight_partial(0)
    arrive(around1)
    conv(1, 3)
    q2 = weight_rows(1, p2)
    gfield_ref[...] = (grad_hidden + mix_back(0)).astype(BF16)
    q1 = weight_rows(0, p1)
    r2 = weight_bands(1, q2)
    r1 = weight_bands(0, q1)
    for layer, ref, got in ((1, g2_ref, r2), (0, g1_ref, r1)):
        for group in got:
            arrive(group)
        for h in range(2):
            ref[:, :, h * 128 : (h + 1) * 128] = fin[layer, h]
    for copy in sent:
        copy.wait_send()


def deliver(*refs):
    count = len(refs) // 2
    for src, dst in zip(refs[:count], refs[count:]):
        dst[...] = src[...]


def local(activation, basis_table, lat_depth, lon_extent, weight_one, weight_two, cotangent):
    vmem = pl.BlockSpec(memory_space=pltpu.VMEM)
    hbm = pl.BlockSpec(memory_space=pltpu.HBM)
    field = jax.ShapeDtypeStruct((CELLS, CH), BF16)
    grad = jax.ShapeDtypeStruct((BASIS, 8, CH), F32)
    shapes = (field, field, grad, grad)
    results = pl.pallas_call(
        kernel,
        out_shape=shapes,
        in_specs=[hbm] * 7,
        out_specs=(vmem,) * 4,
        scratch_shapes=[
            pltpu.VMEM((BASIS, 5, 17, GRID), BF16),
            pltpu.SMEM((GRID,), jnp.int32),
            pltpu.SMEM((GRID,), jnp.int32),
            pltpu.VMEM((CELLS, CH), BF16),
            pltpu.VMEM((BASIS, 128, GRID), F32),
            pltpu.VMEM((ROWS + 4, BASIS, 8, 128), F32),
            pltpu.VMEM((8, BASIS, 16, 256), F32),
            pltpu.VMEM((2, BASIS, CELLS, EXT), BF16),
            pltpu.VMEM((4, EXT, CH), BF16),
            pltpu.VMEM((2, 2, NX, NY, BASIS, 8, 128), BF16),
            pltpu.VMEM((2, BASIS, CH, CH), BF16),
            pltpu.VMEM((BASIS, CELLS, CH), BF16),
            pltpu.VMEM((2, CH, EXT), BF16),
            pltpu.VMEM((2, NX, 64, EXT), BF16),
            pltpu.VMEM((2, NX, 2, BASIS, 64, CELLS), BF16),
            pltpu.VMEM((2, NX, 2, CELLS, 128), BF16),
            pltpu.VMEM((2, NY, BASIS, 8, 128), BF16),
            pltpu.VMEM((2, NY, BASIS, 8, 128), BF16),
            pltpu.VMEM((2, BASIS, 8, 128), BF16),
            pltpu.VMEM((2, NZ, BASIS, 8, 128), BF16),
            pltpu.VMEM((2, 2, BASIS, 8, 128), F32),
            pltpu.VMEM((CELLS, CH), F32),
            pltpu.SemaphoreType.DMA((SLOTS,)),
            pltpu.SemaphoreType.DMA((SLOTS,)),
            pltpu.SemaphoreType.DMA((7,)),
        ],
        compiler_params=pltpu.CompilerParams(
            collective_id=0, has_side_effects=True, vmem_limit_bytes=63 * 1024 * 1024
        ),
        cost_estimate=pl.CostEstimate(flops=10**9, bytes_accessed=10**7, transcendentals=10**5),
    )(
        activation.reshape(CELLS, CH),
        jnp.transpose(basis_table, (0, 2, 3, 1)),
        lat_depth,
        lon_extent,
        weight_one,
        weight_two,
        cotangent.reshape(CELLS, CH),
    )
    out, grad_field, grad_one, grad_two = pl.pallas_call(
        deliver,
        out_shape=shapes,
        in_specs=[vmem] * 4,
        out_specs=(vmem,) * 4,
    )(*results)
    block = (ROWS, COLS, CH)
    return out.reshape(block), grad_field.reshape(block), grad_one, grad_two


def solution(mesh):
    field = P("lat", "lon", None)
    weight = P(None, "lon", None)
    return jax.shard_map(
        local,
        mesh=mesh,
        in_specs=(field, P(), P(), P(), weight, weight, field),
        out_specs=(field, field, weight, weight),
        check_vma=False,
    )
```
